32 devices in a mesh: seq: 8 (over z, y), chan: 4 (over x, core).
Axes of the slice: x: 2, y: 2, z: 4, core: 2. Of those that a mesh axis runs over, the one named last changes fastest.
Arguments:
- targets: int32 [8192], P('seq'), may hold values from 0 to 4
- resid: bfloat16 [8192, 2560], P('seq', 'chan'), may hold values from -6 to 6
- w_gate_in: bfloat16 [2560, 2560], P('seq', 'chan'), may hold values from -0.125 to 0.125
- w_x_in: bfloat16 [2560, 2560], P('seq', 'chan'), may hold values from -0.125 to 0.125
- conv_weight: float32 [4, 2560], P(None, 'chan'), may hold values from -3 to 3
- conv_bias: float32 [2560], P('chan'), may hold values from -3 to 3
- skip_d: float32 [40], P('chan'), may hold values from 0.5 to 2
- norm_gain: float32 [2560], P('chan'), may hold values from 0.1 to 1.9
- w_out: bfloat16 [2560, 2560], P('seq', 'chan'), may hold values from -0.125 to 0.125
- w_head: bfloat16 [2560, 16], P('chan'), may hold values from -0.375 to 0.375
Outputs:
- new_resid: bfloat16 [8192, 2560], P('seq', 'chan')
- grad_gate_in: float32 [2560, 2560], P('seq', 'chan')
- grad_x_in: float32 [2560, 2560], P('seq', 'chan')
- grad_out: float32 [2560, 2560], P('seq', 'chan')
- grad_head: float32 [2560, 16], P('chan')
- grad_conv_weight: float32 [4, 2560], P(None, 'chan')
- grad_conv_bias: float32 [2560], P('chan')
- grad_skip: float32 [40], P('chan')
- grad_gain: float32 [2560], P('chan')
The draws below stay inside these ranges and needn't reach their ends.
All inputs are finite; a program needn't handle non-finite values.
Results may differ from the reference program's by a relative error of at most 0.035.
Values may be sent and summed in bfloat16 or wider, within the bound.
No kernel may reach another device: no remote copies, remote signals or barrier semaphores. Data moves between devices by JAX's collectives and lax.ppermute only.
A program may use at most 128 MiB of HBM per device.

```python
import math
import jax
import jax.numpy as jnp
import numpy as np
from jax import lax

DMODEL = 2560
HEADS = 40
HEADDIM = 64
KERNEL = 4
VOCAB = 16
INNER = 2560
TOKENS = 8192
N_CHAN = 4


def with_ends(array, stream_key, smallest, high):
    place = [jax.random.randint(jax.random.fold_in(stream_key, axis), (), 0, length) for axis, length in enumerate(array.shape)]
    longest = array.shape.index(max(array.shape))
    neighbour = place[:longest] + [(place[longest] + 1) % array.shape[longest]] + place[longest + 1:]
    return array.at[tuple(place)].set(smallest).at[tuple(neighbour)].set(high)


def levels(rng, extent, split, least, top_value):
    factor_of, own = 1.0, jax.random.fold_in(rng, 6)
    for position, blocks in split:
        heights = jnp.exp(jax.random.uniform(jax.random.fold_in(own, position), (blocks,), jnp.float32, least / len(split), top_value / len(split)))
        factor_of = factor_of * jnp.repeat(heights, extent[position] // blocks).reshape([-1 if axis == position else 1 for axis in range(len(extent))])
    return factor_of


def cumulative_ranks(count, skew):
    portions = [(1 << 20) // math.isqrt(standing ** skew) + 1 for standing in range(1, count + 1)]
    deviation = 1 + sum(portions) // (1 << 30)
    return np.cumsum(np.array([max(1, weight // deviation) for weight in portions]))


def ranked_ids(rng, dims, count, skew):
    table = cumulative_ranks(count, skew)
    pick = jax.random.randint(jax.random.fold_in(rng, 1), dims, 0, int(table[count - 1]))
    rank = jnp.searchsorted(jnp.asarray(table, jnp.int32), pick, side="right")
    return jax.random.permutation(jax.random.fold_in(rng, 2), count)[rank].astype(jnp.int32)


def scatter_about(rng, extent, spread, reach, shards=(), held_as=jnp.bfloat16):
    result = spread * jax.random.normal(rng, extent, jnp.float32)
    if shards:
        result = result * levels(rng, extent, shards, -0.22, 0.18)
    return jnp.clip(result, -reach, reach).astype(held_as)


def setup_inputs(seed: int = 0) -> dict:
    key_of = jax.random.split(jax.random.key(seed), 11)
    targets = with_ends(ranked_ids(key_of[0], (TOKENS,), 5, 1), jax.random.fold_in(key_of[0], 3), 0, 4).astype(jnp.int32)
    resid = scatter_about(key_of[1], (TOKENS, DMODEL), 1.0, 6.0, ((0, 8), (1, 4)))
    w_gate_in = scatter_about(key_of[2], (DMODEL, INNER), DMODEL ** -0.5, 0.125, ((0, 8), (1, 4)))
    w_x_in = scatter_about(key_of[3], (DMODEL, INNER), DMODEL ** -0.5, 0.125, ((0, 8), (1, 4)))
    conv_weight = scatter_about(key_of[4], (KERNEL, INNER), 0.5, 3.0, ((1, 4),), jnp.float32)
    conv_bias = scatter_about(key_of[5], (INNER,), 0.5, 3.0, ((0, 4),), jnp.float32)
    skip_d = jnp.clip(jnp.exp(math.log(2.0) - 1.3862944 * jax.random.uniform(key_of[6], (HEADS,), jnp.float32) ** levels(key_of[6], (HEADS,), ((0, 4),), -0.2, 0.2)), 0.5, 2.0)
    norm_gain = jnp.clip(1.0 + 0.18 * jax.random.normal(key_of[7], (INNER,), jnp.float32), 0.1, 1.9)
    w_out = scatter_about(key_of[8], (INNER, DMODEL), INNER ** -0.5, 0.125, ((0, 8), (1, 4)))
    w_head = scatter_about(key_of[9], (DMODEL, VOCAB), (DMODEL // 9) ** -0.5, 0.375, ((0, 4),))
    return {"targets": targets, "resid": resid, "w_gate_in": w_gate_in, "w_x_in": w_x_in, "conv_weight": conv_weight, "conv_bias": conv_bias, "skip_d": skip_d, "norm_gain": norm_gain, "w_out": w_out, "w_head": w_head}


def slope(value, sig):
    return sig * (1.0 + value * (1.0 - sig))

def reference(targets, resid, w_gate_in, w_x_in, conv_weight, conv_bias, skip_d, norm_gain, w_out, w_head):
    f32 = jnp.float32
    bf16 = jnp.bfloat16
    halo_rows = KERNEL - 1
    gate_pre = jnp.dot(resid, w_gate_in, preferred_element_type=f32).astype(bf16)
    x_pre = jnp.dot(resid, w_x_in, preferred_element_type=f32).astype(bf16)
    padded = jnp.concatenate([jnp.zeros((halo_rows, INNER), bf16), x_pre], axis=0).astype(f32)
    conv_out = jnp.zeros((TOKENS, INNER), f32) + conv_bias
    for offset in range(KERNEL):
        conv_out = conv_out + conv_weight[offset] * padded[offset:offset + TOKENS]
    sig_conv = jax.nn.sigmoid(conv_out)
    active = conv_out * sig_conv
    gate_f32 = gate_pre.astype(f32)
    sig_gate = jax.nn.sigmoid(gate_f32)
    silu_gate = gate_f32 * sig_gate
    head_scale = jnp.repeat(skip_d, HEADDIM)
    gated = active * head_scale * silu_gate
    inverse = lax.rsqrt(lax.optimization_barrier(jnp.sum(gated * gated, axis=1)) / INNER + 1e-05)
    normed = (gated * inverse[:, None] * norm_gain).astype(bf16)
    new_resid = (resid.astype(f32) + jnp.dot(normed, w_out, preferred_element_type=f32)).astype(bf16)
    logits = jnp.dot(new_resid, w_head, preferred_element_type=f32)
    raised = jnp.exp(logits)
    probs = raised / lax.optimization_barrier(jnp.sum(raised, axis=1, keepdims=True))
    onehot = (targets[:, None] == jnp.arange(VOCAB, dtype=jnp.int32)[None, :]).astype(f32)
    dlogit = (probs - onehot) * (4.0 / jnp.sqrt(jnp.asarray(TOKENS, f32)))
    grad_head = jnp.dot(new_resid.astype(f32).T, dlogit, precision=lax.Precision.HIGHEST)
    dresid = jnp.dot(dlogit, w_head.astype(f32).T, precision=lax.Precision.HIGHEST).astype(bf16)
    grad_out = jnp.dot(normed.T, dresid, preferred_element_type=f32)
    block = DMODEL // N_CHAN
    dnormed = jnp.zeros((TOKENS, INNER), f32)
    for part in range(N_CHAN):
        term = jnp.dot(dresid[:, part * block:(part + 1) * block], w_out[:, part * block:(part + 1) * block].T, preferred_element_type=f32)
        rounded = lax.optimization_barrier(term.astype(bf16))
        dnormed = dnormed + rounded.astype(f32)
    dot_gn = lax.optimization_barrier(jnp.sum(gated * norm_gain * dnormed, axis=1))
    dgated = inverse[:, None] * norm_gain * dnormed - gated * (inverse ** 3 * dot_gn / INNER)[:, None]
    grad_gain = lax.optimization_barrier(jnp.sum(dnormed * gated * inverse[:, None], axis=0))
    grad_skip = lax.optimization_barrier(jnp.sum(dgated * active * silu_gate, axis=0)).reshape(HEADS, HEADDIM).sum(axis=1)
    dgate = (dgated * active * head_scale * slope(gate_f32, sig_gate)).astype(bf16)
    dconv = dgated * head_scale * silu_gate * slope(conv_out, sig_conv)
    grad_conv_bias = lax.optimization_barrier(jnp.sum(dconv, axis=0))
    grad_conv_weight = jnp.stack([lax.optimization_barrier(jnp.sum(dconv * padded[offset:offset + TOKENS], axis=0)) for offset in range(KERNEL)])
    dpadded = jnp.concatenate([dconv, jnp.zeros((halo_rows, INNER), f32)], axis=0)
    dx_sum = jnp.zeros((TOKENS, INNER), f32)
    for offset in range(KERNEL):
        dx_sum = dx_sum + conv_weight[offset] * dpadded[halo_rows - offset:halo_rows - offset + TOKENS]
    dx_pre = dx_sum.astype(bf16)
    grad_gate_in = jnp.dot(resid.T, dgate, preferred_element_type=f32)
    grad_x_in = jnp.dot(resid.T, dx_pre, preferred_element_type=f32)
    return (new_resid, grad_gate_in, grad_x_in, grad_out, grad_head, grad_conv_weight, grad_conv_bias, grad_skip, grad_gain)
```

```python
import jax
import jax.numpy as jnp
from jax import lax
from jax.sharding import PartitionSpec as P

HEADDIM = 64
KERNEL = 4
VOCAB = 16
INNER = 2560
f32 = jnp.float32
bf16 = jnp.bfloat16
HI = lax.Precision.HIGHEST


def slope(value, sig):
    return sig * (1.0 + value * (1.0 - sig))


def xor_sum(value, axis):
    size = lax.axis_size(axis)
    bit = 1
    while bit < size:
        value = value + lax.ppermute(value, axis, [(i, i ^ bit) for i in range(size)])
        bit *= 2
    return value


def seq_factors():
    slow = 4
    return slow, lax.axis_size("seq") // slow


def move_slow(value, by):
    slow, fast = seq_factors()
    pairs = [(a * fast + b, ((a + by) % slow) * fast + b) for a in range(slow) for b in range(fast)]
    return lax.ppermute(value, "seq", pairs)


def move_fast(value, by):
    slow, fast = seq_factors()
    pairs = [(a * fast + b, a * fast + (b + by) % fast) for a in range(slow) for b in range(fast)]
    return lax.ppermute(value, "seq", pairs)


def shifted(array, by):
    length = lax.axis_size("seq")
    return lax.ppermute(array, "seq", [(i, i + by) for i in range(length) if 0 <= i + by < length])


def gather_rows(shard):
    slow, fast = seq_factors()
    me = lax.axis_index("seq")
    a, b = me // fast, me % fast
    rows = shard.shape[0]
    out = jnp.zeros((slow * fast * rows, shard.shape[1]), shard.dtype)
    own = [shard] + [move_slow(shard, k) for k in range(1, slow)]
    for k, block in enumerate(own):
        for j in range(fast):
            piece = block if j == 0 else move_fast(block, j)
            source = ((a - k) % slow) * fast + (b - j) % fast
            out = lax.dynamic_update_slice(out, piece, (source * rows, 0))
    return out


def gather_chan(shard):
    size = lax.axis_size("chan")
    me = lax.axis_index("chan")
    x_size = size // 2
    cols = shard.shape[1]
    out = jnp.zeros((shard.shape[0], size * cols), shard.dtype)
    for k in range(x_size):
        block = shard
        if k:
            pairs = [(i, ((i // 2 + k) % x_size) * 2 + i % 2) for i in range(size)]
            block = lax.ppermute(shard, "chan", pairs)
        other = lax.ppermute(block, "chan", [(i, i ^ 1) for i in range(size)])
        x_from = (me // 2 - k) % x_size
        out = lax.dynamic_update_slice(out, block, (0, (x_from * 2 + me % 2) * cols))
        out = lax.dynamic_update_slice(out, other, (0, (x_from * 2 + 1 - me % 2) * cols))
    return out


def scatter_rows(grad):
    slow, fast = seq_factors()
    me = lax.axis_index("seq")
    a, b = me // fast, me % fast
    rows = grad.shape[0] // (slow * fast)

    def block(k, j):
        dest = ((a + k) % slow) * fast + (b + j) % fast
        return lax.dynamic_slice_in_dim(grad, dest * rows, rows, 0)

    total = 0.0
    for k in list(range(1, slow)) + [0]:
        part = block(k, 0).astype(f32)
        for j in range(1, fast):
            part = part + move_fast(block(k, j), j).astype(f32)
        if k:
            part = move_slow(part.astype(bf16), k).astype(f32)
        total = total + part
    return total


def inner_rows(left, right):
    return lax.dot_general(
        left, right, (((0,), (0,)), ((), ())), preferred_element_type=f32
    )


def per_device(
    targets, resid, w_gate_in, w_x_in, conv_weight, conv_bias, skip_d, norm_gain, w_out, w_head
):
    tok_rows = resid.shape[0]
    seq_count = lax.axis_size("seq")
    local_inner = w_gate_in.shape[1]
    w_rows = w_out.shape[0]
    halo = KERNEL - 1

    features = gather_chan(resid)
    full_gate = gather_rows(w_gate_in)
    full_x = gather_rows(w_x_in)

    head_t = w_head.T
    part_m = lax.dot_general(
        head_t, w_out, (((1,), (1,)), ((), ())), preferred_element_type=f32
    )
    part_r = lax.dot_general(
        head_t, resid, (((1,), (1,)), ((), ())), preferred_element_type=f32
    )
    early = xor_sum(jnp.concatenate([part_m, part_r], axis=1), "chan")
    resid_logits = early[:, w_rows:]
    m_all = lax.all_gather(early[:, :w_rows], "seq", axis=1, tiled=True)
    m_loc = lax.dynamic_slice_in_dim(m_all, lax.axis_index("chan") * local_inner, local_inner, 1)
    gain_m = m_loc * norm_gain[None, :]

    gate_pre = jnp.dot(features, full_gate, preferred_element_type=f32).astype(bf16)
    x_pre = jnp.dot(features, full_x, preferred_element_type=f32).astype(bf16)
    before = shifted(x_pre[tok_rows - halo :], 1)
    padded = jnp.concatenate([before, x_pre], axis=0).astype(f32)
    conv_out = jnp.zeros((tok_rows, local_inner), f32) + conv_bias
    for offset in range(KERNEL):
        conv_out = conv_out + conv_weight[offset] * padded[offset : offset + tok_rows]
    sig_conv = jax.nn.sigmoid(conv_out)
    active = conv_out * sig_conv
    gate_f32 = gate_pre.astype(f32)
    sig_gate = jax.nn.sigmoid(gate_f32)
    silu_gate = gate_f32 * sig_gate
    head_scale = jnp.repeat(skip_d, HEADDIM)
    gated = active * head_scale * silu_gate
    z_part = lax.dot_general(
        gain_m, gated, (((1,), (1,)), ((), ())), precision=HI, preferred_element_type=f32
    )
    sq_part = jnp.sum(gated * gated, axis=1)
    sums = xor_sum(jnp.concatenate([z_part, jnp.broadcast_to(sq_part[None], (8, tok_rows))]), "chan")
    z_all = sums[:VOCAB]
    inverse = lax.rsqrt(sums[VOCAB] / INNER + 1e-05)
    raised = jnp.exp(resid_logits + inverse[None] * z_all)
    probs = raised / jnp.sum(raised, axis=0, keepdims=True)
    onehot = (targets[None, :] == jnp.arange(VOCAB, dtype=jnp.int32)[:, None]).astype(f32)
    loss_weight = 4.0 / jnp.sqrt(jnp.asarray(tok_rows * seq_count, f32))
    dlogit = (probs - onehot) * loss_weight
    dot_gn = jnp.sum(dlogit * z_all, axis=0)
    dnormed = lax.dot_general(
        dlogit, m_loc, (((0,), (0,)), ((), ())), precision=HI, preferred_element_type=f32
    )
    inv = inverse[:, None]
    dgated = inv * norm_gain * dnormed - gated * (inverse**3 * dot_gn / INNER)[:, None]
    gain_local = jnp.sum(dnormed * gated * inv, axis=0)
    skip_local = jnp.sum(dgated * active * silu_gate, axis=0)
    dgate = (dgated * active * head_scale * slope(gate_f32, sig_gate)).astype(bf16)
    grad_gate_in = scatter_rows(inner_rows(features, dgate).astype(bf16))
    dconv = dgated * head_scale * silu_gate * slope(conv_out, sig_conv)
    bias_local = jnp.sum(dconv, axis=0)
    taps_local = jnp.stack(
        [jnp.sum(dconv * padded[offset : offset + tok_rows], axis=0) for offset in range(KERNEL)]
    )
    future = shifted(dconv[:halo], -1)
    dpadded = jnp.concatenate([dconv, future], axis=0)
    dx_sum = jnp.zeros((tok_rows, local_inner), f32)
    for offset in range(KERNEL):
        dx_sum = (
            dx_sum + conv_weight[offset] * dpadded[halo - offset : halo - offset + tok_rows]
        )
    dx_pre = dx_sum.astype(bf16)
    grad_x_in = scatter_rows(inner_rows(features, dx_pre).astype(bf16))

    normed = (gated * inv * norm_gain).astype(bf16)
    out_cols = gather_rows(w_out)
    full_normed = gather_chan(normed)
    new_resid = (
        resid.astype(f32) + jnp.dot(full_normed, out_cols, preferred_element_type=f32)
    ).astype(bf16)
    head_local = lax.dot_general(
        dlogit, new_resid.astype(f32), (((1,), (0,)), ((), ())), precision=HI
    )
    out_local = lax.dot_general(
        dlogit, gated * inv * norm_gain, (((1,), (0,)), ((), ())), precision=HI
    )
    stacked = jnp.concatenate(
        [head_local, out_local, taps_local, bias_local[None], skip_local[None], gain_local[None]], 0
    )
    late = xor_sum(stacked, "seq")
    grad_head = late[:VOCAB].T
    g_all = lax.all_gather(late[VOCAB : 2 * VOCAB], "chan", axis=1, tiled=True)
    g_rows = lax.dynamic_slice_in_dim(g_all, lax.axis_index("seq") * w_rows, w_rows, 1)
    grad_out = lax.dot_general(
        g_rows, head_t.astype(f32), (((0,), (0,)), ((), ())), precision=HI
    )
    rest = late[2 * VOCAB :]
    grad_skip = rest[KERNEL + 1].reshape(-1, HEADDIM).sum(axis=1)
    return (
        new_resid,
        grad_gate_in,
        grad_x_in,
        grad_out,
        grad_head,
        rest[:KERNEL],
        rest[KERNEL],
        grad_skip,
        rest[KERNEL + 2],
    )


def solution(mesh):
    return jax.shard_map(
        per_device,
        mesh=mesh,
        in_specs=(
            P("seq"),
            P("seq", "chan"),
            P("seq", "chan"),
            P("seq", "chan"),
            P(None, "chan"),
            P("chan"),
            P("chan"),
            P("chan"),
            P("seq", "chan"),
            P("chan", None),
        ),
        out_specs=(
            P("seq", "chan"),
            P("seq", "chan"),
            P("seq", "chan"),
            P("seq", "chan"),
            P("chan", None),
            P(None, "chan"),
            P("chan"),
            P("chan"),
            P("chan"),
        ),
        check_vma=False,
    )
```

```python
import functools

import jax
import jax.numpy as jnp
from jax import lax
from jax.experimental import pallas as pl
from jax.experimental.pallas import tpu as pltpu
from jax.sharding import PartitionSpec as P

HEADDIM = 64
KERNEL = 4
VOCAB = 16
INNER = 2560
f32 = jnp.float32
bf16 = jnp.bfloat16
HI = lax.Precision.HIGHEST
LIGHT = pl.CostEstimate(flops=1, bytes_accessed=1, transcendentals=0)
MIB = 1024 * 1024
PROJ_VMEM = 48 * MIB


def slope(value, sig):
    return sig * (1.0 + value * (1.0 - sig))


def after(value, *others):
    return lax.optimization_barrier((value,) + others)[0]


def flip(value, axis, bit):
    return lax.ppermute(value, axis, [(i, i ^ bit) for i in range(lax.axis_size(axis))])


def xor_sum(value, axis):
    bit = 1
    while bit < lax.axis_size(axis):
        value = value + flip(value, axis, bit)
        bit *= 2
    return value


def xor_gather(value, axis, least=1):
    size = lax.axis_size(axis)
    blocks = {0: value}
    bit = size // 2
    while bit >= least:
        for j in list(blocks):
            blocks[j | bit] = flip(blocks[j], axis, bit)
        bit //= 2
    return [blocks[j] for j in range(0, size, least)]


def seq_factors():
    slow = 4
    return slow, lax.axis_size("seq") // slow


def move_slow(value, by):
    slow, fast = seq_factors()
    pairs = [(a * fast + b, ((a + by) % slow) * fast + b) for a in range(slow) for b in range(fast)]
    return lax.ppermute(value, "seq", pairs)


def move_fast(value, by):
    slow, fast = seq_factors()
    pairs = [(a * fast + b, a * fast + (b + by) % fast) for a in range(slow) for b in range(fast)]
    return lax.ppermute(value, "seq", pairs)


def shifted(array, by):
    length = lax.axis_size("seq")
    return lax.ppermute(array, "seq", [(i, i + by) for i in range(length) if 0 <= i + by < length])


def sync(*groups):
    flat = lax.optimization_barrier(tuple(value for group in groups for value in group))
    out, at = [], 0
    for group in groups:
        out.append(list(flat[at : at + len(group)]))
        at += len(group)
    return out


def to_fast(block):
    return [move_fast(block, j) for j in range(1, seq_factors()[1])]


def slow_total(own, came):
    even, odd = own + came[1], came[0] + came[2]
    return even + odd


def gather_sources():
    slow, fast = seq_factors()
    me = lax.axis_index("seq")
    a, b = me // fast, me % fast
    return [((a - k) % slow) * fast + (b - j) % fast for k in range(slow) for j in range(fast)]


def picked(pieces, sources, wanted):
    return sum(jnp.where(source == wanted, piece, 0.0) for source, piece in zip(sources, pieces))


def turn_kernel(n_feat, *refs):
    for j in range(n_feat):
        refs[n_feat][j] = refs[j][...].T


def turned(feats):
    tok, depth = feats[0].shape
    n_feat = len(feats)
    tile = 256
    return pl.pallas_call(
        functools.partial(turn_kernel, n_feat),
        out_shape=jax.ShapeDtypeStruct((n_feat, depth, tok), bf16),
        grid=(tok // tile,),
        in_specs=[pl.BlockSpec((tile, depth), lambda i: (i, 0))] * n_feat,
        out_specs=pl.BlockSpec((n_feat, depth, tile), lambda i: (0, 0, i)),
        compiler_params=pltpu.CompilerParams(vmem_limit_bytes=12 * MIB),
        cost_estimate=LIGHT,
    )(*feats)


def proj_kernel(n_feat, n_shard, idx, *refs):
    feats = refs[:n_feat]
    shards = refs[n_feat : n_feat + n_shard]
    out = refs[n_feat + n_shard]
    fbuf, wbuf, total, fsem, wsem = refs[n_feat + n_shard + 1 :]
    rows = shards[0].shape[0]
    depth = feats[0].shape[1]

    def w_copy(s):
        at = pl.ds(pl.multiple_of(idx[n_feat + s] * rows, 16), rows)
        return pltpu.make_async_copy(shards[s], wbuf.at[at], wsem.at[s])

    def f_copy(j):
        return pltpu.make_async_copy(feats[j], fbuf.at[j], fsem.at[j])

    f_copy(0).start()
    for s in range(n_shard):
        w_copy(s).start()
    for j in range(1, n_feat):
        f_copy(j).start()
    for s in range(n_shard):
        w_copy(s).wait()
    for j in range(n_feat):
        f_copy(j).wait()
        at = pl.ds(pl.multiple_of(idx[j] * depth, 16), depth)
        term = jnp.dot(fbuf[j], wbuf[at, :], preferred_element_type=f32)
        if j == 0:
            total[...] = term
        elif j < n_feat - 1:
            total[...] += term
        else:
            out[...] = (total[...] + term).astype(out.dtype)


def proj(feats, shards, idx):
    tok, depth = feats[0].shape
    rows, cols = shards[0].shape
    n_feat, n_shard = len(feats), len(shards)
    any_spec = pl.BlockSpec(memory_space=pltpu.HBM)
    return pl.pallas_call(
        functools.partial(proj_kernel, n_feat, n_shard),
        out_shape=jax.ShapeDtypeStruct((tok, cols), bf16),
        in_specs=[pl.BlockSpec(memory_space=pltpu.SMEM)] + [any_spec] * (n_feat + n_shard),
        out_specs=pl.BlockSpec(memory_space=pltpu.VMEM),
        scratch_shapes=[
            pltpu.VMEM((n_feat, tok, depth), bf16),
            pltpu.VMEM((n_shard * rows, cols), bf16),
            pltpu.VMEM((tok, cols), f32),
            pltpu.SemaphoreType.DMA((n_feat,)),
            pltpu.SemaphoreType.DMA((n_shard,)),
        ],
        compiler_params=pltpu.CompilerParams(vmem_limit_bytes=PROJ_VMEM),
        cost_estimate=LIGHT,
    )(idx, *feats, *shards)


def blocks_kernel(n_out, idx, lhs, rhs, *outs):
    for i in range(n_out):

        @pl.when(pl.program_id(0) == i)
        def _():
            total = jnp.dot(lhs[0], rhs[...], preferred_element_type=f32)
            outs[i][...] = total.astype(bf16)


def block_grads(feat_t, rhs, places, begin, count, rows):
    tok = feat_t.shape[2]
    cols = rhs.shape[1]
    return pl.pallas_call(
        functools.partial(blocks_kernel, count),
        out_shape=[jax.ShapeDtypeStruct((rows, cols), bf16)] * count,
        grid_spec=pltpu.PrefetchScalarGridSpec(
            num_scalar_prefetch=1,
            grid=(count,),
            in_specs=[
                pl.BlockSpec((1, rows, tok), lambda i, idx: (idx[2 * (begin + i)], idx[2 * (begin + i) + 1], 0)),
                pl.BlockSpec((tok, cols), lambda i, idx: (0, 0)),
            ],
            out_specs=[pl.BlockSpec((rows, cols), lambda i, idx: (0, 0))] * count,
        ),
        compiler_params=pltpu.CompilerParams(vmem_limit_bytes=16 * MIB),
        cost_estimate=LIGHT,
    )(places, feat_t, rhs)


def dest_places(keys, rows, depth):
    slow, fast = seq_factors()
    me = lax.axis_index("seq")
    per_feat = depth // rows
    out = []
    for k, j in keys:
        dest = ((me // fast + k) % slow) * fast + (me % fast + j) % fast
        out += [(dest // per_feat) ^ lax.axis_index("chan"), dest % per_feat]
    return out


def slow_order():
    return [2, 1, 3, 0]


def far_blocks(feat_t, rhs, rows):
    fast = seq_factors()[1]
    return {
        (k, j): block_grad(feat_t, rhs, dest_block(feat_t, rows, k, j), [], rows, bf16)
        for k in slow_order()
        for j in range(1, fast)
    }


def per_device(
    targets, resid, w_gate_in, w_x_in, conv_weight, conv_bias, skip_d, norm_gain, w_out, w_head
):
    tok_rows = resid.shape[0]
    seq_count = lax.axis_size("seq")
    chan_count = lax.axis_size("chan")
    chan = lax.axis_index("chan")
    local_inner = w_gate_in.shape[1]
    w_rows = w_out.shape[0]
    halo = KERNEL - 1

    sources = gather_sources()
    slow, fast = seq_factors()
    order = slow_order()
    far = [(k, j) for k in order for j in range(1, fast)]
    near = [(k, 0) for k in order]
    idx = [chan ^ j for j in range(chan_count)] + sources
    idx += dest_places(far + near, w_rows, resid.shape[1])
    idx = jnp.concatenate([jnp.reshape(i, (1,)) for i in idx]).astype(jnp.int32)
    n_idx = chan_count + seq_count


    gate_now, x_now = w_gate_in, w_x_in
    gate_shards, x_shards = [], []
    extra = [idx]
    for k in range(slow - 1):
        gate_shards.append(gate_now)
        x_shards.append(x_now)
        came = [move_slow(gate_now, 1), move_slow(x_now, 1)]
        gate_fast, x_fast = to_fast(gate_now), to_fast(x_now)
        if k == 0:
            feats = xor_gather(resid, "chan", 2)
        if k == 1:
            head_t = after(w_head.T, gate_now)
            part_m = lax.dot_general(
                head_t, w_out, (((1,), (1,)), ((), ())), preferred_element_type=f32
            )
            part_r = lax.dot_general(
                head_t, resid, (((1,), (1,)), ((), ())), preferred_element_type=f32
            )
            early = jnp.concatenate([part_m, part_r], axis=1)
            early = early + flip(early, "chan", 1)
            extra = [early] + feats
        if k == 2:
            bit = 2
            while bit < chan_count:
                early = early + flip(early, "chan", bit)
                bit *= 2
            full = []
            for block in feats:
                full += [block, flip(block, "chan", 1)]
            extra = [early] + full
        came, gate_fast, x_fast, extra = sync(came, gate_fast, x_fast, extra)
        gate_now, x_now = came
        gate_shards += gate_fast
        x_shards += x_fast
        if k == 0:
            idx = extra[0]
        if k > 0:
            early, feats = extra[0], extra[1:]
    gate_shards.append(gate_now)
    x_shards.append(x_now)
    gate_fast, x_fast = to_fast(gate_now), to_fast(x_now)
    own_m, resid_logits = early[:, :w_rows], early[:, w_rows:]
    fast_m = to_fast(own_m)
    feat_t = turned(feats)
    out_slow = [after(w_out, gate_now)]
    out_slow.append(move_slow(out_slow[0], 1))
    gate_fast, fast_m, out_slow, held = sync(
        gate_fast, fast_m, out_slow, [gate_shards[0], feat_t]
    )
    feat_t = held[1]
    pair_m = jnp.concatenate([own_m] + fast_m, axis=1)
    moved_m = [move_slow(pair_m, k) for k in range(1, slow)]
    gate_pre = proj(feats, [held[0]] + gate_shards[1:] + gate_fast, idx)
    out_slow.append(move_slow(out_slow[1], 1))
    x_fast, moved_m, out_slow, held = sync(
        x_fast, moved_m, out_slow, [x_shards[0], gate_pre, pair_m]
    )
    gate_pre, pair_m = held[1:]
    x_pre = proj(feats, [held[0]] + x_shards[1:] + x_fast, idx)
    out_slow.append(move_slow(out_slow[2], 1))
    out_shards = [[out_slow[k]] + to_fast(out_slow[k]) for k in range(2)]

    all_m = jnp.concatenate([pair_m] + moved_m, axis=1)
    per_chan = local_inner // w_rows
    pieces = [all_m[:, i * w_rows : (i + 1) * w_rows] for i in range(seq_count)]
    m_loc = jnp.concatenate(
        [picked(pieces, sources, chan * per_chan + i) for i in range(per_chan)], axis=1
    )
    gain_m = m_loc * norm_gain[None, :]

    before = shifted(x_pre[tok_rows - halo :], 1)
    padded = jnp.concatenate([before, x_pre], axis=0).astype(f32)
    conv_out = jnp.zeros((tok_rows, local_inner), f32) + conv_bias
    for offset in range(KERNEL):
        conv_out = conv_out + conv_weight[offset] * padded[offset : offset + tok_rows]
    sig_conv = jax.nn.sigmoid(conv_out)
    active = conv_out * sig_conv
    gate_f32 = gate_pre.astype(f32)
    sig_gate = jax.nn.sigmoid(gate_f32)
    silu_gate = gate_f32 * sig_gate
    head_scale = jnp.repeat(skip_d, HEADDIM)
    gated = active * head_scale * silu_gate
    z_part = lax.dot_general(
        gain_m, gated, (((1,), (1,)), ((), ())), precision=HI, preferred_element_type=f32
    )
    sq_part = jnp.sum(gated * gated, axis=1)
    sq_part = jnp.sum(gated * gated, axis=1)
    z_part = after(z_part, *out_shards[1:fast])
    normed_all = xor_gather((gated * norm_gain).astype(bf16), "chan")
    sums = jnp.concatenate([z_part, jnp.broadcast_to(sq_part[None], (8, tok_rows))])
    held, out_shards[0], out_shards[1], out_slow = sync(
        [sums], out_shards[0], out_shards[1], out_slow
    )
    sums = xor_sum(held[0], "chan")
    for k in range(2, slow):
        out_shards.append([out_slow[k]] + to_fast(out_slow[k]))
    normed = (gated * norm_gain).astype(bf16)
    normed_x = xor_gather(after(normed, sums), "chan", 2)
    z_all = sums[:VOCAB]
    inverse = lax.rsqrt(sums[VOCAB] / INNER + 1e-05)
    raised = jnp.exp(resid_logits + inverse[None] * z_all)
    probs = raised / jnp.sum(raised, axis=0, keepdims=True)
    onehot = (targets[None, :] == jnp.arange(VOCAB, dtype=jnp.int32)[:, None]).astype(f32)
    loss_weight = 4.0 / jnp.sqrt(jnp.asarray(tok_rows * seq_count, f32))
    dlogit = (probs - onehot) * loss_weight
    dot_gn = jnp.sum(dlogit * z_all, axis=0)
    dnormed = lax.dot_general(
        dlogit, m_loc, (((0,), (0,)), ((), ())), precision=HI, preferred_element_type=f32
    )
    inv = inverse[:, None]
    dgated = inv * norm_gain * dnormed - gated * (inverse**3 * dot_gn / INNER)[:, None]
    gain_local = jnp.sum(dnormed * gated * inv, axis=0)
    skip_local = jnp.sum(dgated * active * silu_gate, axis=0)
    dgate = (dgated * active * head_scale * slope(gate_f32, sig_gate)).astype(bf16)
    dconv = dgated * head_scale * silu_gate * slope(conv_out, sig_conv)
    bias_local = jnp.sum(dconv, axis=0)
    taps_local = jnp.stack(
        [jnp.sum(dconv * padded[offset : offset + tok_rows], axis=0) for offset in range(KERNEL)]
    )
    future = shifted(dconv[:halo], -1)

    def grads(rhs, keys):
        begin = n_idx // 2 + (0 if keys is far else len(far))
        return dict(zip(keys, block_grads(feat_t, rhs, idx, begin, len(keys), w_rows)))

    def send_fast(blocks, ks):
        return [move_fast(blocks[k, j], j) for k in ks for j in range(1, fast)]

    def total_of(own, came, k, ks):
        at = ks.index(k) * (fast - 1)
        return own[k, 0].astype(f32) + sum(b.astype(f32) for b in came[at : at + fast - 1])

    def send_slow(own, came, k, ks):
        return move_slow(total_of(own, came, k, ks).astype(bf16), k)

    first, second = order[:2], order[2:]

    gate = grads(dgate, far)
    held = sync([gate[key] for key in far], [future, dconv, dlogit, dgate], *out_shards[2:])
    gate = dict(zip(far, held[0]))
    future, dconv, dlogit, dgate = held[1]
    out_shards[2:] = held[2:]

    came = send_fast(gate, first)
    dpadded = jnp.concatenate([dconv, future], axis=0)
    dx_sum = jnp.zeros((tok_rows, local_inner), f32)
    for offset in range(KERNEL):
        dx_sum = (
            dx_sum + conv_weight[offset] * dpadded[halo - offset : halo - offset + tok_rows]
        )
    dx_pre = dx_sum.astype(bf16)
    gate_own = grads(dgate, near)
    x = grads(dx_pre, far)
    out_local = lax.dot_general(
        dlogit, gated * inv * norm_gain, (((1,), (0,)), ((), ())), precision=HI
    )
    mid = jnp.concatenate(
        [out_local, taps_local, bias_local[None], skip_local[None], gain_local[None]], 0
    )
    gate_first, normed_x, mid, held = sync(
        came,
        normed_x,
        [mid],
        [gate[key] for key in far] + [x[key] for key in far] + [gate_own[key] for key in near],
    )
    mid = mid[0]
    gate = dict(zip(far, held))
    x = dict(zip(far, held[len(far) :]))
    gate_own = dict(zip(near, held[2 * len(far) :]))

    came = send_fast(gate, second)
    gate_slow = [send_slow(gate_own, gate_first, k, first) for k in first]
    mid_came = to_fast(mid)
    normed_all = []
    for block in normed_x:
        normed_all += [block, flip(block, "chan", 1)]
    raw = proj(normed_all, [block for group in out_shards for block in group], idx)
    gate_second, mid_came, x_far, held = sync(
        came, mid_came, [x[key] for key in far], [raw, dx_pre]
    )
    raw, dx_pre = held
    x = dict(zip(far, x_far))
    mid = mid + sum(mid_came)

    came = send_fast(x, first)
    gate_slow.append(send_slow(gate_own, gate_second, second[0], second))
    mid_came = [move_slow(mid, k) for k in range(1, slow)]
    x_own = grads(dx_pre, near)
    new_resid = (resid.astype(f32) + inv * raw.astype(f32)).astype(bf16)
    head_local = lax.dot_general(
        dlogit, new_resid.astype(f32), (((1,), (0,)), ((), ())), precision=HI
    )
    head_came = to_fast(head_local)
    x_first, gate_slow[:2], head_came, mid_came, held = sync(
        came,
        gate_slow[:2],
        head_came,
        mid_came,
        [x[key] for key in far] + [x_own[key] for key in near],
    )
    x = dict(zip(far, held))
    x_own = dict(zip(near, held[len(far) :]))
    head_local = head_local + sum(head_came)

    came = send_fast(x, second)
    x_slow = [send_slow(x_own, x_first, k, first) for k in first]
    head_came = [move_slow(head_local, k) for k in range(1, slow)]
    mid = slow_total(mid, mid_came)
    g_pieces = xor_gather(mid[:VOCAB], "chan")
    x_second, g_pieces, gate_slow = sync(came, g_pieces, gate_slow)

    x_slow.append(send_slow(x_own, x_second, second[0], second))
    head_local = slow_total(head_local, head_came)
    grad_gate_in = total_of(gate_own, gate_second, 0, second) + sum(
        block.astype(f32) for block in gate_slow
    )
    grad_x_in = total_of(x_own, x_second, 0, second) + sum(
        block.astype(f32) for block in x_slow
    )
    grad_head = head_local.T
    seq = lax.axis_index("seq")
    g_chan = picked(g_pieces, [chan ^ j for j in range(chan_count)], seq // per_chan)
    g_rows = lax.dynamic_slice_in_dim(g_chan, (seq % per_chan) * w_rows, w_rows, 1)
    grad_out = lax.dot_general(
        g_rows, w_head.T.astype(f32), (((0,), (0,)), ((), ())), precision=HI
    )
    tail = mid[VOCAB:]
    grad_skip = tail[KERNEL + 1].reshape(-1, HEADDIM).sum(axis=1)
    return (
        new_resid,
        grad_gate_in,
        grad_x_in,
        grad_out,
        grad_head,
        tail[:KERNEL],
        tail[KERNEL],
        grad_skip,
        tail[KERNEL + 2],
    )


def solution(mesh):
    return jax.shard_map(
        per_device,
        mesh=mesh,
        in_specs=(
            P("seq"),
            P("seq", "chan"),
            P("seq", "chan"),
            P("seq", "chan"),
            P(None, "chan"),
            P("chan"),
            P("chan"),
            P("chan"),
            P("seq", "chan"),
            P("chan", None),
        ),
        out_specs=(
            P("seq", "chan"),
            P("seq", "chan"),
            P("seq", "chan"),
            P("seq", "chan"),
            P("chan", None),
            P(None, "chan"),
            P("chan"),
            P("chan"),
            P("chan"),
        ),
        check_vma=False,
    )
```

```python
import functools

import jax
import jax.numpy as jnp
from jax import lax
from jax.experimental import pallas as pl
from jax.experimental.pallas import tpu as pltpu
from jax.sharding import PartitionSpec as P

HEADDIM = 64
KERNEL = 4
VOCAB = 16
INNER = 2560
f32 = jnp.float32
bf16 = jnp.bfloat16
HI = lax.Precision.HIGHEST
LIGHT = pl.CostEstimate(flops=1, bytes_accessed=1, transcendentals=0)
MIB = 1024 * 1024
PROJ_VMEM = 58 * MIB


def slope(value, sig):
    return sig * (1.0 + value * (1.0 - sig))


def after(value, *others):
    return lax.optimization_barrier((value,) + others)[0]


def flip(value, axis, bit):
    return lax.ppermute(value, axis, [(i, i ^ bit) for i in range(lax.axis_size(axis))])


def xor_sum(value, axis):
    bit = 1
    while bit < lax.axis_size(axis):
        value = value + flip(value, axis, bit)
        bit *= 2
    return value


def xor_gather(value, axis, least=1):
    size = lax.axis_size(axis)
    blocks = {0: value}
    bit = size // 2
    while bit >= least:
        for j in list(blocks):
            blocks[j | bit] = flip(blocks[j], axis, bit)
        bit //= 2
    return [blocks[j] for j in range(0, size, least)]


def seq_factors():
    slow = 4
    return slow, lax.axis_size("seq") // slow


def move_slow(value, by):
    slow, fast = seq_factors()
    pairs = [(a * fast + b, ((a + by) % slow) * fast + b) for a in range(slow) for b in range(fast)]
    return lax.ppermute(value, "seq", pairs)


def move_fast(value, by):
    slow, fast = seq_factors()
    pairs = [(a * fast + b, a * fast + (b + by) % fast) for a in range(slow) for b in range(fast)]
    return lax.ppermute(value, "seq", pairs)


def shifted(array, by):
    length = lax.axis_size("seq")
    return lax.ppermute(array, "seq", [(i, i + by) for i in range(length) if 0 <= i + by < length])


def sync(*groups):
    flat = lax.optimization_barrier(tuple(value for group in groups for value in group))
    out, at = [], 0
    for group in groups:
        out.append(list(flat[at : at + len(group)]))
        at += len(group)
    return out


def to_fast(block):
    return [move_fast(block, j) for j in range(1, seq_factors()[1])]


def slow_total(own, came):
    even, odd = own + came[1], came[0] + came[2]
    return even + odd


def gather_sources():
    slow, fast = seq_factors()
    me = lax.axis_index("seq")
    a, b = me // fast, me % fast
    return [((a - k) % slow) * fast + (b - j) % fast for k in range(slow) for j in range(fast)]


def picked(pieces, sources, wanted):
    return sum(jnp.where(source == wanted, piece, 0.0) for source, piece in zip(sources, pieces))


def turn_kernel(n_feat, *refs):
    for j in range(n_feat):
        refs[n_feat][j] = refs[j][...].T


def turned(feats):
    tok, depth = feats[0].shape
    n_feat = len(feats)
    tile = 256
    return pl.pallas_call(
        functools.partial(turn_kernel, n_feat),
        out_shape=jax.ShapeDtypeStruct((n_feat, depth, tok), bf16),
        grid=(tok // tile,),
        in_specs=[pl.BlockSpec((tile, depth), lambda i: (i, 0))] * n_feat,
        out_specs=pl.BlockSpec((n_feat, depth, tile), lambda i: (0, 0, i)),
        compiler_params=pltpu.CompilerParams(vmem_limit_bytes=PROJ_VMEM),
        cost_estimate=LIGHT,
    )(*feats)


def proj_kernel(n_feat, counts, idx, *refs):
    feats = refs[:n_feat]
    shards = refs[n_feat : n_feat + len(counts)]
    out = refs[n_feat + len(counts)]
    fbuf, wbuf, fsem, wsem = refs[n_feat + len(counts) + 1 :]
    rows = shards[0].shape[1]
    tok, depth = feats[0].shape
    joined = len(fbuf.shape) == 2
    n_tile = fsem.shape[1]
    tile = tok // n_tile

    def f_copy(j, t):
        at = pl.ds(t * tile, tile)
        to = fbuf.at[at, pl.ds(j * depth, depth)] if joined else fbuf.at[j, at]
        return pltpu.make_async_copy(feats[j].at[at], to, fsem.at[j, t])

    copies = []
    for shard, places in zip(shards, counts):
        for i, s in enumerate(places):
            place = pl.ds(pl.multiple_of(idx[n_feat + s] * rows, 16), rows)
            copies.append(pltpu.make_async_copy(shard.at[i], wbuf.at[place], wsem.at[s]))
    for copy in copies:
        copy.start()
    for t in range(n_tile):
        for j in range(n_feat):
            f_copy(j, t).start()
    for copy in copies:
        copy.wait()
    for t in range(n_tile):
        at = pl.ds(t * tile, tile)
        for j in range(n_feat):
            f_copy(j, t).wait()
        if joined:
            total = jnp.dot(fbuf[at, :], wbuf[...], preferred_element_type=f32)
        else:
            total = jnp.zeros((tile, wbuf.shape[1]), f32)
            for j in range(n_feat):
                part = wbuf[j * depth : (j + 1) * depth, :]
                total += jnp.dot(fbuf[j, at, :], part, preferred_element_type=f32)
        out[at, :] = total.astype(out.dtype)


def proj(feats, shards, counts, idx):
    tok, depth = feats[0].shape
    rows, cols = shards[0].shape[1:]
    n_feat, n_shard = len(feats), sum(len(places) for places in counts)
    any_spec = pl.BlockSpec(memory_space=pltpu.HBM)
    return pl.pallas_call(
        functools.partial(proj_kernel, n_feat, counts),
        out_shape=jax.ShapeDtypeStruct((tok, cols), bf16),
        in_specs=[pl.BlockSpec(memory_space=pltpu.SMEM)] + [any_spec] * (n_feat + len(shards)),
        out_specs=pl.BlockSpec(memory_space=pltpu.VMEM),
        scratch_shapes=[
            pltpu.VMEM((tok, n_feat * depth) if depth % 128 == 0 else (n_feat, tok, depth), bf16),
            pltpu.VMEM((n_shard * rows, cols), bf16),
            pltpu.SemaphoreType.DMA((n_feat, 2)),
            pltpu.SemaphoreType.DMA((n_shard,)),
        ],
        compiler_params=pltpu.CompilerParams(vmem_limit_bytes=PROJ_VMEM),
        cost_estimate=LIGHT,
    )(idx, *feats, *shards)


def group_kernel(n_feat, n_fast, n_use, first, ats, idx, *refs):
    part = None if first else refs[0]
    refs = refs if first else refs[1:]
    n_shard, n_block = n_fast * len(ats), n_use * len(ats)
    feats = refs[:n_feat]
    shards = refs[n_feat : n_feat + n_shard]
    outs = refs[n_feat + n_shard : -4]
    fbuf, wbuf, fsem, wsem = refs[-4:]
    count, rows = shards[0].shape[:2]
    depth = fbuf.shape[2]
    tile = outs[0].shape[-2]
    step = pl.program_id(0)

    def w_copy(i):
        at = ats[i // n_fast] + n_use + i % n_fast
        place = pl.multiple_of((i // n_fast * n_fast + idx[at]) * rows, 16)
        return pltpu.make_async_copy(shards[i], wbuf.at[:, pl.ds(place, rows)], wsem.at[i])

    @pl.when(step == 0)
    def _():
        for m in range(n_block):
            for j in range(n_feat):

                @pl.when(idx[ats[m // n_use] + m % n_use] == j)
                def _():
                    pltpu.make_async_copy(feats[j], fbuf.at[m], fsem.at[m]).start()

        for i in range(n_shard):
            w_copy(i).start()
        for i in range(n_shard):
            w_copy(i).wait()
        for m in range(n_block):
            pltpu.make_async_copy(feats[0], fbuf.at[m], fsem.at[m]).wait()

    here = pl.ds(pl.multiple_of(step * tile, tile), tile)
    for w in range(count):
        total = None if first else part[w]
        for m in range(n_block):
            rhs = wbuf[w, m * depth : (m + 1) * depth, :]
            term = jnp.dot(fbuf[m, here, :], rhs, preferred_element_type=f32)
            total = term if total is None else total + term
        if len(outs) == 1:
            outs[0][w] = total
        else:
            outs[w][...] = total.astype(bf16)


def add_groups(part, feats, shards, idx, ats, n_use, final):
    count, rows, cols = shards[0].shape
    tok, depth = feats[0].shape
    n_feat, n_shard, n_block = len(feats), len(shards), n_use * len(ats)
    tile = tok // 4
    any_spec = pl.BlockSpec(memory_space=pltpu.HBM)
    whole = pl.BlockSpec((count, tile, cols), lambda i, idx: (0, i, 0))
    if final:
        out_shape = [jax.ShapeDtypeStruct((tok, cols), bf16)] * count
        out_specs = [pl.BlockSpec((tile, cols), lambda i, idx: (i, 0))] * count
    else:
        out_shape = [jax.ShapeDtypeStruct((count, tok, cols), f32)]
        out_specs = [whole]
    parts = [] if part is None else [part]
    return pl.pallas_call(
        functools.partial(group_kernel, n_feat, n_shard // len(ats), n_use, part is None, ats),
        out_shape=out_shape,
        grid_spec=pltpu.PrefetchScalarGridSpec(
            num_scalar_prefetch=1,
            grid=(tok // tile,),
            in_specs=[whole] * len(parts) + [any_spec] * (n_feat + n_shard),
            out_specs=out_specs,
            scratch_shapes=[
                pltpu.VMEM((n_block, tok, depth), bf16),
                pltpu.VMEM((count, n_shard * rows, cols), bf16),
                pltpu.SemaphoreType.DMA((n_block,)),
                pltpu.SemaphoreType.DMA((n_shard,)),
            ],
        ),
        compiler_params=pltpu.CompilerParams(vmem_limit_bytes=PROJ_VMEM),
        cost_estimate=LIGHT,
    )(idx, *parts, *feats, *shards)


def blocks_kernel(sizes, idx, lhs, rhs, *outs):
    at = 0
    for out, size in zip(outs, sizes):
        for i in range(size):

            @pl.when(pl.program_id(0) == at)
            def _():
                total = jnp.dot(lhs[0], rhs[...], preferred_element_type=f32)
                out[i] = total.astype(bf16)

            at += 1


def block_grads(feat_t, rhs, places, begin, sizes, rows):
    tok = feat_t.shape[2]
    cols = rhs.shape[1]

    def place(i, idx):
        return (idx[2 * (begin + i)], idx[2 * (begin + i) + 1], 0)

    return pl.pallas_call(
        functools.partial(blocks_kernel, sizes),
        out_shape=[jax.ShapeDtypeStruct((size, rows, cols), bf16) for size in sizes],
        grid_spec=pltpu.PrefetchScalarGridSpec(
            num_scalar_prefetch=1,
            grid=(sum(sizes),),
            in_specs=[
                pl.BlockSpec((1, rows, tok), place),
                pl.BlockSpec((tok, cols), lambda i, idx: (0, 0)),
            ],
            out_specs=[
                pl.BlockSpec((size, rows, cols), lambda i, idx: (0, 0, 0)) for size in sizes
            ],
        ),
        compiler_params=pltpu.CompilerParams(vmem_limit_bytes=16 * MIB),
        cost_estimate=LIGHT,
    )(places, feat_t, rhs)


def dest_places(keys, rows, depth):
    slow, fast = seq_factors()
    me = lax.axis_index("seq")
    per_feat = depth // rows
    out = []
    for k, j in keys:
        dest = ((me // fast + k) % slow) * fast + (me % fast + j) % fast
        out += [(dest // per_feat) ^ lax.axis_index("chan"), dest % per_feat]
    return out


def slow_order():
    return [1, 3, 2, 0]


def per_device(
    targets, resid, w_gate_in, w_x_in, conv_weight, conv_bias, skip_d, norm_gain, w_out, w_head
):
    tok_rows = resid.shape[0]
    seq_count = lax.axis_size("seq")
    chan_count = lax.axis_size("chan")
    chan = lax.axis_index("chan")
    local_inner = w_gate_in.shape[1]
    w_rows = w_out.shape[0]
    halo = KERNEL - 1

    sources = gather_sources()
    slow, fast = seq_factors()
    order = slow_order()
    first, second = order[:2], order[2:]
    far = [(k, j) for pair in (first, second) for j in range(1, fast) for k in pair]
    near = [(k, 0) for k in order]
    per_feat = resid.shape[1] // w_rows
    idx = [chan ^ j for j in range(chan_count)]
    idx += [((i // per_feat) ^ chan) * per_feat + i % per_feat for i in sources]
    idx += dest_places(far + near, w_rows, resid.shape[1])
    n_idx = chan_count + seq_count
    n_use = fast // per_feat
    group_at = []
    for k in range(slow):
        group_at.append(len(idx))
        mine = sources[k * fast : (k + 1) * fast]
        idx += [(mine[0] // fast * n_use + m) ^ chan for m in range(n_use)]
        idx += [source % fast for source in mine]
    idx = jnp.concatenate([jnp.reshape(i, (1,)) for i in idx]).astype(jnp.int32)

    now = jnp.stack([w_gate_in, w_x_in])
    shards = []
    extra = [idx]
    for k in range(slow - 1):
        shards.append(now)
        came = [move_slow(now, 1)]
        came_fast = to_fast(now)
        if k == 0:
            feats = xor_gather(resid, "chan", 2)
        if k == 1:
            head_t = after(w_head.T, now)
            part_m = lax.dot_general(
                head_t, w_out, (((1,), (1,)), ((), ())), preferred_element_type=f32
            )
            part_r = lax.dot_general(
                head_t, resid, (((1,), (1,)), ((), ())), preferred_element_type=f32
            )
            early = jnp.concatenate([part_m, part_r], axis=1)
            early = early + flip(early, "chan", 1)
            extra = [early] + feats
        if k == 2:
            bit = 2
            while bit < chan_count:
                early = early + flip(early, "chan", bit)
                bit *= 2
            full = []
            for block in feats:
                full += [block, flip(block, "chan", 1)]
            feats = full
            feat_t = turned(feats)
            part = add_groups(
                None, feats, shards[: 2 * fast], idx, group_at[:2], n_use, False
            )[0]
            own_m, resid_logits = early[:, :w_rows], early[:, w_rows:]
            own_m = after(own_m, part)
            pair_m = jnp.concatenate([own_m] + to_fast(own_m), axis=1)
            extra = [pair_m, resid_logits, feat_t, part] + feats
        came, came_fast, extra = sync(came, came_fast, extra)
        now = came[0]
        shards += came_fast
        if k == 0:
            idx = extra[0]
        if k == 1:
            early, feats = extra[0], extra[1:]
    pair_m, resid_logits, feat_t, part = extra[:4]
    feats = extra[4:]
    shards.append(now)
    came_fast = to_fast(now)
    moved_m = [move_slow(pair_m, k) for k in range(1, slow)]
    out_first = after(w_out, now)
    out_pair = jnp.stack([out_first, move_slow(out_first, 1)])
    came_fast, moved_m, held = sync(came_fast, moved_m, [now, out_pair])
    now, out_pair = held
    out_pair_fast = to_fast(out_pair)
    out_far = [move_slow(out_pair[1], 1), move_slow(out_first, 3)]
    last = shards[2 * fast : 3 * fast] + [now] + came_fast
    gate_pre, x_pre = add_groups(part, feats, last, idx, group_at[2:], n_use, True)

    all_m = jnp.concatenate([pair_m] + moved_m, axis=1)
    per_chan = per_feat
    pieces = [all_m[:, i * w_rows : (i + 1) * w_rows] for i in range(seq_count)]
    m_loc = jnp.concatenate(
        [picked(pieces, sources, chan * per_chan + i) for i in range(per_chan)], axis=1
    )
    gain_m = m_loc * norm_gain[None, :]

    before = shifted(x_pre[tok_rows - halo :], 1)
    padded = jnp.concatenate([before, x_pre], axis=0).astype(f32)
    conv_out = jnp.zeros((tok_rows, local_inner), f32) + conv_bias
    for offset in range(KERNEL):
        conv_out = conv_out + conv_weight[offset] * padded[offset : offset + tok_rows]
    sig_conv = jax.nn.sigmoid(conv_out)
    active = conv_out * sig_conv
    gate_f32 = gate_pre.astype(f32)
    sig_gate = jax.nn.sigmoid(gate_f32)
    silu_gate = gate_f32 * sig_gate
    head_scale = jnp.repeat(skip_d, HEADDIM)
    gated = active * head_scale * silu_gate
    z_part = lax.dot_general(
        gain_m, gated, (((1,), (1,)), ((), ())), precision=HI, preferred_element_type=f32
    )
    sq_part = jnp.sum(gated * gated, axis=1)
    sums = jnp.concatenate([z_part, jnp.broadcast_to(sq_part[None], (8, tok_rows))])
    held, out_pair_fast, out_far = sync([sums], out_pair_fast, out_far)
    sums = xor_sum(held[0], "chan")
    out_far = jnp.stack(out_far)
    out_far_fast = to_fast(out_far)
    normed = (gated * norm_gain).astype(bf16)
    normed_x = xor_gather(after(normed, sums), "chan", 2)
    z_all = sums[:VOCAB]
    inverse = lax.rsqrt(sums[VOCAB] / INNER + 1e-05)
    raised = jnp.exp(resid_logits + inverse[None] * z_all)
    probs = raised / jnp.sum(raised, axis=0, keepdims=True)
    onehot = (targets[None, :] == jnp.arange(VOCAB, dtype=jnp.int32)[:, None]).astype(f32)
    loss_weight = 4.0 / jnp.sqrt(jnp.asarray(tok_rows * seq_count, f32))
    dlogit = (probs - onehot) * loss_weight
    dot_gn = jnp.sum(dlogit * z_all, axis=0)
    dnormed = lax.dot_general(
        dlogit, m_loc, (((0,), (0,)), ((), ())), precision=HI, preferred_element_type=f32
    )
    inv = inverse[:, None]
    dgated = inv * norm_gain * dnormed - gated * (inverse**3 * dot_gn / INNER)[:, None]
    gain_local = jnp.sum(dnormed * gated * inv, axis=0)
    skip_local = jnp.sum(dgated * active * silu_gate, axis=0)
    dgate = (dgated * active * head_scale * slope(gate_f32, sig_gate)).astype(bf16)
    dconv = dgated * head_scale * silu_gate * slope(conv_out, sig_conv)
    bias_local = jnp.sum(dconv, axis=0)
    taps_local = jnp.stack(
        [jnp.sum(dconv * padded[offset : offset + tok_rows], axis=0) for offset in range(KERNEL)]
    )
    future = shifted(dconv[:halo], -1)

    def far_grads(rhs):
        sizes = [2] * (2 * fast - 2)
        out = block_grads(feat_t, rhs, idx, n_idx // 2, sizes, w_rows)
        return out[: fast - 1], out[fast - 1 :]

    def near_grads(rhs):
        return block_grads(feat_t, rhs, idx, n_idx // 2 + len(far), [1] * slow, w_rows)

    def send_fast(blocks):
        return [move_fast(block, j) for j, block in enumerate(blocks, 1)]

    def total_of(own, came, i):
        return own[0].astype(f32) + sum(block[i].astype(f32) for block in came)

    def send_slow(own, came, i, k):
        return move_slow(total_of(own, came, i).astype(bf16), k)

    far_gate = far_grads(dgate)
    gate_first, gate_second, held, out_far_fast = sync(
        *far_gate, [future, dconv, dlogit, dgate], out_far_fast
    )
    future, dconv, dlogit, dgate = held

    came = send_fast(gate_first)
    dpadded = jnp.concatenate([dconv, future], axis=0)
    dx_sum = jnp.zeros((tok_rows, local_inner), f32)
    for offset in range(KERNEL):
        dx_sum = (
            dx_sum + conv_weight[offset] * dpadded[halo - offset : halo - offset + tok_rows]
        )
    dx_pre = dx_sum.astype(bf16)
    out_local = lax.dot_general(
        dlogit, gated * inv * norm_gain, (((1,), (0,)), ((), ())), precision=HI
    )
    mid = jnp.concatenate(
        [out_local, taps_local, bias_local[None], skip_local[None], gain_local[None]], 0
    )
    gate_own = near_grads(dgate)
    x_first, x_second = far_grads(dx_pre)
    mid = after(mid, x_first[0], gate_own[0])
    mid_came = [move_slow(mid, k) for k in range(1, slow)]
    gate_first, gate_second, x_first, x_second, gate_own, normed_x, mid_came, held = sync(
        came, gate_second, x_first, x_second, gate_own, normed_x, mid_came, [dx_pre, mid]
    )
    dx_pre, mid = held
    mid = slow_total(mid, mid_came)

    came = send_fast(gate_second)
    gate_slow = [send_slow(gate_own[i], gate_first, i, first[i]) for i in range(2)]
    normed_all = []
    for block in normed_x:
        normed_all += [block, flip(block, "chan", 1)]
    out_shards = [out_pair] + out_pair_fast + [out_far] + out_far_fast
    counts = [[k * fast + j for k in ks] for ks in ((0, 1), (2, 3)) for j in range(fast)]
    raw = proj(normed_all, out_shards, counts, idx)
    gate_second, gate_slow, x_first, x_second, held = sync(
        came, gate_slow, x_first, x_second, [raw, dx_pre]
    )
    raw, dx_pre = held

    came = send_fast(x_first)
    gate_slow.append(send_slow(gate_own[2], gate_second, 0, second[0]))
    x_own = near_grads(dx_pre)
    new_resid = (resid.astype(f32) + inv * raw.astype(f32)).astype(bf16)
    head_local = lax.dot_general(
        dlogit, new_resid.astype(f32), (((1,), (0,)), ((), ())), precision=HI
    )
    mid_came = to_fast(after(mid, x_own[0]))
    head_local = after(head_local, x_own[0])
    head_came = [move_slow(head_local, k) for k in range(1, slow)]
    x_first, x_second, x_own, gate_slow, mid_came, head_came, held = sync(
        came, x_second, x_own, gate_slow, mid_came, head_came, [mid, head_local]
    )
    mid, head_local = held
    mid = mid + sum(mid_came)
    head_local = slow_total(head_local, head_came)

    came = send_fast(x_second)
    x_terms = [total_of(x_own[i], x_first, i).astype(bf16) for i in range(2)]
    x_slow = [move_slow(x_terms[i], first[i]) for i in range(2)]
    head_came = to_fast(after(head_local, *x_terms))
    g_pieces = xor_gather(after(mid[:VOCAB], *x_terms), "chan")
    x_second, x_slow, head_came, g_pieces = sync(came, x_slow, head_came, g_pieces)

    x_slow.append(send_slow(x_own[2], x_second, 0, second[0]))
    head_local = head_local + sum(head_came)
    grad_gate_in = total_of(gate_own[3], gate_second, 1) + sum(
        block.astype(f32) for block in gate_slow
    )
    grad_x_in = total_of(x_own[3], x_second, 1) + sum(block.astype(f32) for block in x_slow)
    grad_head = head_local.T
    seq = lax.axis_index("seq")
    g_chan = picked(g_pieces, [chan ^ j for j in range(chan_count)], seq // per_chan)
    g_rows = lax.dynamic_slice_in_dim(g_chan, (seq % per_chan) * w_rows, w_rows, 1)
    grad_out = lax.dot_general(
        g_rows, w_head.T.astype(f32), (((0,), (0,)), ((), ())), precision=HI
    )
    tail = mid[VOCAB:]
    grad_skip = tail[KERNEL + 1].reshape(-1, HEADDIM).sum(axis=1)
    return (
        new_resid,
        grad_gate_in,
        grad_x_in,
        grad_out,
        grad_head,
        tail[:KERNEL],
        tail[KERNEL],
        grad_skip,
        tail[KERNEL + 2],
    )


def solution(mesh):
    return jax.shard_map(
        per_device,
        mesh=mesh,
        in_specs=(
            P("seq"),
            P("seq", "chan"),
            P("seq", "chan"),
            P("seq", "chan"),
            P(None, "chan"),
            P("chan"),
            P("chan"),
            P("chan"),
            P("seq", "chan"),
            P("chan", None),
        ),
        out_specs=(
            P("seq", "chan"),
            P("seq", "chan"),
            P("seq", "chan"),
            P("seq", "chan"),
            P("chan", None),
            P(None, "chan"),
            P("chan"),
            P("chan"),
            P("chan"),
        ),
        check_vma=False,
    )
```

```python
import functools
import math

import jax
import jax.numpy as jnp
from jax import lax
from jax.experimental import pallas as pl
from jax.experimental.pallas import tpu as pltpu
from jax.sharding import PartitionSpec as P

HEADDIM = 64
KERNEL = 4
VOCAB = 16
INNER = 2560
f32 = jnp.float32
bf16 = jnp.bfloat16
HI = lax.Precision.HIGHEST
EDGE = 16
LIGHT = pl.CostEstimate(flops=1, bytes_accessed=1, transcendentals=0)
MIB = 1024 * 1024
PROJ_VMEM = 58 * MIB


def slope(value, sig):
    return sig * (1.0 + value * (1.0 - sig))


def after(value, *others):
    return lax.optimization_barrier((value,) + others)[0]


def flip(value, axis, bit):
    return lax.ppermute(value, axis, [(i, i ^ bit) for i in range(lax.axis_size(axis))])


def xor_sum(value, axis):
    bit = 1
    while bit < lax.axis_size(axis):
        value = value + flip(value, axis, bit)
        bit *= 2
    return value


def xor_gather(value, axis, least=1):
    size = lax.axis_size(axis)
    blocks = {0: value}
    bit = size // 2
    while bit >= least:
        for j in list(blocks):
            blocks[j | bit] = flip(blocks[j], axis, bit)
        bit //= 2
    return [blocks[j] for j in range(0, size, least)]


def seq_factors():
    slow = 4
    return slow, lax.axis_size("seq") // slow


def move_slow(value, by):
    slow, fast = seq_factors()
    pairs = [(a * fast + b, ((a + by) % slow) * fast + b) for a in range(slow) for b in range(fast)]
    return lax.ppermute(value, "seq", pairs)


def move_fast(value, by):
    slow, fast = seq_factors()
    pairs = [(a * fast + b, a * fast + (b + by) % fast) for a in range(slow) for b in range(fast)]
    return lax.ppermute(value, "seq", pairs)


def shifted(array, by):
    length = lax.axis_size("seq")
    return lax.ppermute(array, "seq", [(i, i + by) for i in range(length) if 0 <= i + by < length])


def sync(*groups):
    flat = lax.optimization_barrier(tuple(value for group in groups for value in group))
    out, at = [], 0
    for group in groups:
        out.append(list(flat[at : at + len(group)]))
        at += len(group)
    return out


def to_fast(block):
    return [move_fast(block, j) for j in range(1, seq_factors()[1])]


def slow_total(own, came):
    even, odd = own + came[1], came[0] + came[2]
    return even + odd


def gather_sources():
    slow, fast = seq_factors()
    me = lax.axis_index("seq")
    a, b = me // fast, me % fast
    return [((a - k) % slow) * fast + (b - j) % fast for k in range(slow) for j in range(fast)]


def picked(pieces, sources, wanted):
    return sum(jnp.where(source == wanted, piece, 0.0) for source, piece in zip(sources, pieces))


def turn_kernel(n_feat, *refs):
    for j in range(n_feat):
        refs[n_feat][j] = refs[j][...].T


def turned(feats):
    tok, depth = feats[0].shape
    n_feat = len(feats)
    tile = 256
    return pl.pallas_call(
        functools.partial(turn_kernel, n_feat),
        out_shape=jax.ShapeDtypeStruct((n_feat, depth, tok), bf16),
        grid=(tok // tile,),
        in_specs=[pl.BlockSpec((tile, depth), lambda i: (i, 0))] * n_feat,
        out_specs=pl.BlockSpec((n_feat, depth, tile), lambda i: (0, 0, i)),
        compiler_params=pltpu.CompilerParams(vmem_limit_bytes=PROJ_VMEM),
        cost_estimate=LIGHT,
    )(*feats)


def proj_kernel(n_feat, counts, idx, *refs):
    feats = refs[:n_feat]
    shards = refs[n_feat : n_feat + len(counts)]
    out = refs[n_feat + len(counts)]
    fbuf, wbuf, fsem, wsem = refs[n_feat + len(counts) + 1 :]
    rows = shards[0].shape[1]
    tok, depth = feats[0].shape
    joined = len(fbuf.shape) == 2
    n_tile = fsem.shape[1]
    tile = tok // n_tile

    def f_copy(j, t):
        at = pl.ds(t * tile, tile)
        to = fbuf.at[at, pl.ds(j * depth, depth)] if joined else fbuf.at[j, at]
        return pltpu.make_async_copy(feats[j].at[at], to, fsem.at[j, t])

    copies = []
    for shard, places in zip(shards, counts):
        for i, s in enumerate(places):
            place = pl.ds(pl.multiple_of(idx[n_feat + s] * rows, 16), rows)
            copies.append(pltpu.make_async_copy(shard.at[i], wbuf.at[place], wsem.at[s]))
    for copy in copies:
        copy.start()
    for t in range(n_tile):
        for j in range(n_feat):
            f_copy(j, t).start()
    for copy in copies:
        copy.wait()
    for t in range(n_tile):
        at = pl.ds(t * tile, tile)
        for j in range(n_feat):
            f_copy(j, t).wait()
        if joined:
            total = jnp.dot(fbuf[at, :], wbuf[...], preferred_element_type=f32)
        else:
            total = jnp.zeros((tile, wbuf.shape[1]), f32)
            for j in range(n_feat):
                part = wbuf[j * depth : (j + 1) * depth, :]
                total += jnp.dot(fbuf[j, at, :], part, preferred_element_type=f32)
        out[at, :] = total.astype(out.dtype)


def proj(feats, shards, counts, idx):
    tok, depth = feats[0].shape
    rows, cols = shards[0].shape[1:]
    n_feat, n_shard = len(feats), sum(len(places) for places in counts)
    any_spec = pl.BlockSpec(memory_space=pltpu.HBM)
    return pl.pallas_call(
        functools.partial(proj_kernel, n_feat, counts),
        out_shape=jax.ShapeDtypeStruct((tok, cols), bf16),
        in_specs=[pl.BlockSpec(memory_space=pltpu.SMEM)] + [any_spec] * (n_feat + len(shards)),
        out_specs=pl.BlockSpec(memory_space=pltpu.VMEM),
        scratch_shapes=[
            pltpu.VMEM((tok, n_feat * depth) if depth % 128 == 0 else (n_feat, tok, depth), bf16),
            pltpu.VMEM((n_shard * rows, cols), bf16),
            pltpu.SemaphoreType.DMA((n_feat, 2)),
            pltpu.SemaphoreType.DMA((n_shard,)),
        ],
        compiler_params=pltpu.CompilerParams(vmem_limit_bytes=PROJ_VMEM),
        cost_estimate=LIGHT,
    )(idx, *feats, *shards)


def bring(n_feat, n_fast, n_use, ats, idx, feats, edges, shards, bufs):
    fbuf, ebuf, wbuf, fsem, esem, wsem = bufs
    rows = shards[0].shape[1]
    depth = feats[0].shape[1]
    blocks = range(n_use * len(ats))

    def slot(buf, m):
        return buf.at[:, pl.ds(m * depth, depth)] if len(buf.shape) == 2 else buf.at[m]

    def w_copy(i):
        at = ats[i // n_fast] + n_use + i % n_fast
        place = pl.multiple_of((i // n_fast * n_fast + idx[at]) * rows, 16)
        return pltpu.make_async_copy(shards[i], wbuf.at[:, pl.ds(place, rows)], wsem.at[i])

    for m in blocks:
        for j in range(n_feat):

            @pl.when(idx[ats[m // n_use] + m % n_use] == j)
            def _():
                pltpu.make_async_copy(feats[j], slot(fbuf, m), fsem.at[m]).start()
                pltpu.make_async_copy(edges[j], slot(ebuf, m), esem.at[m]).start()

    for i in range(len(shards)):
        w_copy(i).start()
    for i in range(len(shards)):
        w_copy(i).wait()
    for m in blocks:
        pltpu.make_async_copy(edges[0], slot(ebuf, m), esem.at[m]).wait()
        pltpu.make_async_copy(feats[0], slot(fbuf, m), fsem.at[m]).wait()


def product(buf, here, weights):
    if len(buf.shape) == 2:
        return jnp.dot(buf[here, :], weights[...], preferred_element_type=f32)
    depth = buf.shape[2]
    total = None
    for m in range(buf.shape[0]):
        rhs = weights[m * depth : (m + 1) * depth, :]
        term = jnp.dot(buf[m, here, :], rhs, preferred_element_type=f32)
        total = term if total is None else total + term
    return total


def part_kernel(n_feat, n_fast, n_use, ats, more, idx, *refs):
    if more:
        part, part_edge = refs[:2]
        refs = refs[2:]
    n_shard = n_fast * len(ats)
    feats, edges = refs[:n_feat], refs[n_feat : 2 * n_feat]
    shards = refs[2 * n_feat : 2 * n_feat + n_shard]
    out, out_edge = refs[2 * n_feat + n_shard : 2 * n_feat + n_shard + 2]
    bufs = refs[-6:]
    fbuf, ebuf, wbuf = bufs[:3]
    step = pl.program_id(0)
    tile = out.shape[1]

    @pl.when(step == 0)
    def _():
        bring(n_feat, n_fast, n_use, ats, idx, feats, edges, shards, bufs)
        term = product(ebuf, pl.ds(0, EDGE), wbuf.at[1])
        out_edge[...] = term + part_edge[...] if more else term

    here = pl.ds(pl.multiple_of(step * tile, tile), tile)
    for w in range(2):
        term = product(fbuf, here, wbuf.at[w])
        out[w] = term + part[w] if more else term


def front_kernel(n_feat, n_fast, n_use, ats, idx, part, part_edge, params, m_loc, *refs):
    n_shard = n_fast * len(ats)
    feats, edges = refs[:n_feat], refs[n_feat : 2 * n_feat]
    shards = refs[2 * n_feat : 2 * n_feat + n_shard]
    gate_out, x_out, edge_out, z_out = refs[2 * n_feat + n_shard : 2 * n_feat + n_shard + 4]
    xs, zs, ms = refs[-9:-6]
    bufs = refs[-6:]
    fbuf, ebuf, wbuf = bufs[:3]
    step = pl.program_id(0)
    tile = x_out.shape[0]

    @pl.when(step == 0)
    def _():
        bring(n_feat, n_fast, n_use, ats, idx, feats, edges, shards, bufs)
        edge = (part_edge[...] + product(ebuf, pl.ds(0, EDGE), wbuf.at[1])).astype(bf16)
        edge_out[...] = edge
        high, low = halves(m_loc[...])
        ms[...] = jnp.zeros_like(ms)
        ms[0:VOCAB, :] = high
        ms[VOCAB : 2 * VOCAB, :] = low
        xs[0:8, :] = edge.astype(f32)[EDGE - 8 :, :]

    @pl.when(step > 0)
    def _():
        xs[0:8, :] = xs[tile : tile + 8, :]

    here = pl.ds(pl.multiple_of(step * tile, tile), tile)
    x = (part[1] + product(fbuf, here, wbuf.at[1])).astype(bf16)
    x_out[...] = x
    xs[8 : 8 + tile, :] = x.astype(f32)
    gate = (part[0] + product(fbuf, here, wbuf.at[0])).astype(bf16)
    gate_out[...] = gate
    gate = gate.astype(f32)
    conv = params[4:5, :]
    for k in range(KERNEL):
        conv = conv + params[k : k + 1, :] * xs[5 + k : 5 + k + tile, :]
    gated = conv * jax.nn.sigmoid(conv) * params[5:6, :] * (gate * jax.nn.sigmoid(gate))
    normed = (gated * params[6:7, :]).astype(bf16)
    z = lax.dot_general(
        normed, ms[...], (((1,), (1,)), ((), ())), preferred_element_type=f32
    )
    square = jnp.sum(gated * gated, axis=1, keepdims=True)
    lane = lax.broadcasted_iota(jnp.int32, z.shape, 1)
    zs[here, :] = jnp.where(lane == 2 * VOCAB, square, z)

    @pl.when(step == pl.num_programs(0) - 1)
    def _():
        turned_z = zs[...].T
        z_out[0:VOCAB, :] = turned_z[0:VOCAB, :] + turned_z[VOCAB : 2 * VOCAB, :]
        z_out[VOCAB:, :] = turned_z[2 * VOCAB : 2 * VOCAB + 8, :]


def halves(value):
    high = value.astype(bf16)
    return high, (value - high.astype(f32)).astype(bf16)


def in_specs_of(feats, edges, shards):
    return [pl.BlockSpec(memory_space=pltpu.HBM)] * (len(feats) + len(edges) + len(shards))


def buffers_of(feats, shards, n_block):
    tok, depth = feats[0].shape
    count, rows, cols = shards[0].shape
    joined = depth % 128 == 0
    return [
        pltpu.VMEM((tok, n_block * depth) if joined else (n_block, tok, depth), bf16),
        pltpu.VMEM((EDGE, n_block * depth) if joined else (n_block, EDGE, depth), bf16),
        pltpu.VMEM((count, len(shards) * rows, cols), bf16),
        pltpu.SemaphoreType.DMA((n_block,)),
        pltpu.SemaphoreType.DMA((n_block,)),
        pltpu.SemaphoreType.DMA((len(shards),)),
    ]


def partial_products(parts, feats, edges, shards, idx, ats, n_use):
    count, rows, cols = shards[0].shape
    tok = feats[0].shape[0]
    n_fast = len(shards) // len(ats)
    tile = tok // 4
    part_specs = [
        pl.BlockSpec((count, tile, cols), lambda i, idx: (0, i, 0)),
        pl.BlockSpec((EDGE, cols), lambda i, idx: (0, 0)),
    ]
    return pl.pallas_call(
        functools.partial(part_kernel, len(feats), n_fast, n_use, ats, len(parts) > 0),
        out_shape=[
            jax.ShapeDtypeStruct((count, tok, cols), f32),
            jax.ShapeDtypeStruct((EDGE, cols), f32),
        ],
        grid_spec=pltpu.PrefetchScalarGridSpec(
            num_scalar_prefetch=1,
            grid=(tok // tile,),
            in_specs=part_specs[: len(parts)] + in_specs_of(feats, edges, shards),
            out_specs=part_specs,
            scratch_shapes=buffers_of(feats, shards, n_use * len(ats)),
        ),
        compiler_params=pltpu.CompilerParams(vmem_limit_bytes=PROJ_VMEM),
        cost_estimate=LIGHT,
    )(idx, *parts, *feats, *edges, *shards)


def front(part, part_edge, params, m_loc, feats, edges, shards, idx, ats, n_use):
    count, rows, cols = shards[0].shape
    tok = feats[0].shape[0]
    n_fast = len(shards) // len(ats)
    tile = tok // 4
    fixed = [pl.BlockSpec(a.shape, lambda i, idx: (0, 0)) for a in (part_edge, params, m_loc)]
    rows_spec = pl.BlockSpec((tile, cols), lambda i, idx: (i, 0))
    return pl.pallas_call(
        functools.partial(front_kernel, len(feats), n_fast, n_use, ats),
        out_shape=[
            jax.ShapeDtypeStruct((tok, cols), bf16),
            jax.ShapeDtypeStruct((tok, cols), bf16),
            jax.ShapeDtypeStruct((EDGE, cols), bf16),
            jax.ShapeDtypeStruct((VOCAB + 8, tok), f32),
        ],
        grid_spec=pltpu.PrefetchScalarGridSpec(
            num_scalar_prefetch=1,
            grid=(tok // tile,),
            in_specs=[pl.BlockSpec((count, tile, cols), lambda i, idx: (0, i, 0))]
            + fixed
            + in_specs_of(feats, edges, shards),
            out_specs=[
                rows_spec,
                rows_spec,
                pl.BlockSpec((EDGE, cols), lambda i, idx: (0, 0)),
                pl.BlockSpec((VOCAB + 8, tok), lambda i, idx: (0, 0)),
            ],
            scratch_shapes=[
                pltpu.VMEM((tile + 8, cols), f32),
                pltpu.VMEM((tok, 128), f32),
                pltpu.VMEM((128, cols), bf16),
            ]
            + buffers_of(feats, shards, n_use * len(ats)),
        ),
        compiler_params=pltpu.CompilerParams(vmem_limit_bytes=PROJ_VMEM),
        cost_estimate=LIGHT,
    )(idx, part, part_edge, params, m_loc, *feats, *edges, *shards)


def back_kernel(
    weight, n_sum, gate_in, x_in, edge, params, m_loc, resid_logits, targets, *refs
):
    parts = refs[:n_sum]
    dgate_out, dconv_out, normed_out, dlogit_out, acc, square_out, xs = refs[n_sum:]
    step = pl.program_id(0)
    tile = x_in.shape[0]

    @pl.when(step == 0)
    def _():
        acc[...] = jnp.zeros_like(acc)
        xs[0:8, :] = edge[...].astype(f32)[EDGE - 8 :, :]

    @pl.when(step > 0)
    def _():
        xs[0:8, :] = xs[tile : tile + 8, :]

    sums = parts[0][...]
    for other in parts[1:]:
        sums = sums + other[...]
    z = sums[0:VOCAB, :]
    square_out[...] = sums[VOCAB:, :]
    inverse = lax.rsqrt(sums[VOCAB : VOCAB + 1, :] / INNER + 1e-05)
    raised = jnp.exp(resid_logits[...] + inverse * z)
    probs = raised / jnp.sum(raised, axis=0, keepdims=True)
    row = lax.broadcasted_iota(jnp.int32, probs.shape, 0)
    onehot = jnp.where(row == targets[...], 1.0, 0.0)
    dlogit = (probs - onehot) * weight
    dlogit_out[...] = dlogit
    dot_gn = jnp.sum(dlogit * z, axis=0, keepdims=True)
    coef = inverse * inverse * inverse * dot_gn / INNER
    which = lax.broadcasted_iota(jnp.int32, (8, tile), 0)
    columns = jnp.where(which == 0, inverse, coef).T
    inv, coef = columns[:, 0:1], columns[:, 1:2]

    xs[8 : 8 + tile, :] = x_in[...].astype(f32)
    conv = params[4:5, :]
    for k in range(KERNEL):
        conv = conv + params[k : k + 1, :] * xs[5 + k : 5 + k + tile, :]
    scale, gain = params[5:6, :], params[6:7, :]
    sig_conv = jax.nn.sigmoid(conv)
    active = conv * sig_conv
    gate = gate_in[...].astype(f32)
    sig_gate = jax.nn.sigmoid(gate)
    silu_gate = gate * sig_gate
    gated = active * scale * silu_gate
    normed = gated * gain
    normed_out[...] = normed.astype(bf16)
    high, low = halves(dlogit)
    sums_out = jnp.dot(
        jnp.concatenate([high, low], axis=0),
        (normed * inv).astype(bf16),
        preferred_element_type=f32,
    )
    acc[0:VOCAB, :] += sums_out[0:VOCAB, :] + sums_out[VOCAB:, :]
    m_high, m_low = halves(m_loc[...])
    dnormed = lax.dot_general(
        jnp.concatenate([high, high, low], axis=0),
        jnp.concatenate([m_high, m_low, m_high], axis=0),
        (((0,), (0,)), ((), ())),
        preferred_element_type=f32,
    )
    scaled = dnormed * inv
    acc[VOCAB + 6 : VOCAB + 7, :] += jnp.sum(scaled * gated, axis=0, keepdims=True)
    dgated = scaled * gain - gated * coef
    both = dgated * active
    acc[VOCAB + 5 : VOCAB + 6, :] += jnp.sum(both * silu_gate, axis=0, keepdims=True)
    dgate_out[...] = (both * scale * slope(gate, sig_gate)).astype(bf16)
    dconv = dgated * scale * silu_gate * slope(conv, sig_conv)
    dconv_out[...] = dconv
    acc[VOCAB + 4 : VOCAB + 5, :] += jnp.sum(dconv, axis=0, keepdims=True)
    for k in range(KERNEL):
        tap = jnp.sum(dconv * xs[5 + k : 5 + k + tile, :], axis=0, keepdims=True)
        acc[VOCAB + k : VOCAB + k + 1, :] += tap


def back(gate_pre, x_pre, edge, params, m_loc, sums, resid_logits, targets, weight):
    tok, cols = x_pre.shape
    tile = tok // 4
    rows_spec = pl.BlockSpec((tile, cols), lambda i: (i, 0))

    def fixed(a):
        return pl.BlockSpec(a.shape, lambda i: (0, 0))

    def tokens(a):
        return pl.BlockSpec((a.shape[0], tile), lambda i: (0, i))

    return pl.pallas_call(
        functools.partial(back_kernel, weight, len(sums)),
        out_shape=[
            jax.ShapeDtypeStruct((tok, cols), bf16),
            jax.ShapeDtypeStruct((tok, cols), f32),
            jax.ShapeDtypeStruct((tok, cols), bf16),
            jax.ShapeDtypeStruct((VOCAB, tok), f32),
            jax.ShapeDtypeStruct((VOCAB + 8, cols), f32),
            jax.ShapeDtypeStruct((8, tok), f32),
        ],
        grid=(tok // tile,),
        in_specs=[rows_spec, rows_spec, fixed(edge), fixed(params), fixed(m_loc)]
        + [tokens(a) for a in (resid_logits, targets, *sums)],
        out_specs=[
            rows_spec,
            rows_spec,
            rows_spec,
            pl.BlockSpec((VOCAB, tile), lambda i: (0, i)),
            pl.BlockSpec((VOCAB + 8, cols), lambda i: (0, 0)),
            pl.BlockSpec((8, tile), lambda i: (0, i)),
        ],
        scratch_shapes=[pltpu.VMEM((tile + 8, cols), f32)],
        compiler_params=pltpu.CompilerParams(vmem_limit_bytes=PROJ_VMEM),
        cost_estimate=LIGHT,
    )(gate_pre, x_pre, edge, params, m_loc, resid_logits, targets, *sums)


def blocks_kernel(sizes, idx, lhs, rhs, *outs):
    at = 0
    for out, size in zip(outs, sizes):
        for i in range(size):

            @pl.when(pl.program_id(0) == at)
            def _():
                total = jnp.dot(lhs[0], rhs[...], preferred_element_type=f32)
                out[i] = total.astype(bf16)

            at += 1


def block_grads(feat_t, rhs, places, begin, sizes, rows, vmem=16 * MIB):
    tok = feat_t.shape[2]
    cols = rhs.shape[1]

    def place(i, idx):
        return (idx[2 * (begin + i)], idx[2 * (begin + i) + 1], 0)

    return pl.pallas_call(
        functools.partial(blocks_kernel, sizes),
        out_shape=[jax.ShapeDtypeStruct((size, rows, cols), bf16) for size in sizes],
        grid_spec=pltpu.PrefetchScalarGridSpec(
            num_scalar_prefetch=1,
            grid=(sum(sizes),),
            in_specs=[
                pl.BlockSpec((1, rows, tok), place),
                pl.BlockSpec((tok, cols), lambda i, idx: (0, 0)),
            ],
            out_specs=[
                pl.BlockSpec((size, rows, cols), lambda i, idx: (0, 0, 0)) for size in sizes
            ],
        ),
        compiler_params=pltpu.CompilerParams(vmem_limit_bytes=vmem),
        cost_estimate=LIGHT,
    )(places, feat_t, rhs)


def dest_places(keys, rows, depth):
    slow, fast = seq_factors()
    me = lax.axis_index("seq")
    per_feat = depth // rows
    out = []
    for k, j in keys:
        dest = ((me // fast + k) % slow) * fast + (me % fast + j) % fast
        out += [(dest // per_feat) ^ lax.axis_index("chan"), dest % per_feat]
    return out


def slow_order():
    return [1, 3, 2, 0]


def per_device(
    targets, resid, w_gate_in, w_x_in, conv_weight, conv_bias, skip_d, norm_gain, w_out, w_head
):
    tok_rows = resid.shape[0]
    seq_count = lax.axis_size("seq")
    chan_count = lax.axis_size("chan")
    chan = lax.axis_index("chan")
    local_inner = w_gate_in.shape[1]
    w_rows = w_out.shape[0]
    halo = KERNEL - 1

    sources = gather_sources()
    slow, fast = seq_factors()
    order = slow_order()
    first, second = order[:2], order[2:]
    far = [(k, j) for pair in (first, second) for j in range(1, fast) for k in pair]
    near = [(k, 0) for k in order]
    per_feat = resid.shape[1] // w_rows
    idx = [chan ^ j for j in range(chan_count)]
    idx += [((i // per_feat) ^ chan) * per_feat + i % per_feat for i in sources]
    idx += dest_places(far + near, w_rows, resid.shape[1])
    n_idx = chan_count + seq_count
    n_use = fast // per_feat
    group_at = []
    for k in range(slow):
        group_at.append(len(idx))
        mine = sources[k * fast : (k + 1) * fast]
        idx += [(mine[0] // fast * n_use + m) ^ chan for m in range(n_use)]
        idx += [source % fast for source in mine]
    idx = jnp.concatenate([jnp.reshape(i, (1,)) for i in idx]).astype(jnp.int32)

    now = jnp.stack([w_gate_in, w_x_in])
    shards = []
    extra = [idx]
    for k in range(slow - 1):
        shards.append(now)
        came = [move_slow(now, 1)]
        came_fast = to_fast(now)
        if k == 0:
            feats = xor_gather(resid, "chan", 2)
            edge = shifted(resid[tok_rows - EDGE :], 1)
            head_t = w_head.T
            part_m = lax.dot_general(
                head_t, w_out, (((1,), (1,)), ((), ())), preferred_element_type=f32
            )
            part_r = lax.dot_general(
                head_t, resid, (((1,), (1,)), ((), ())), preferred_element_type=f32
            )
            early = jnp.concatenate([part_m, part_r], axis=1)
            early = early + flip(early, "chan", 1)
            extra = [idx, edge, early]
        if k == 1:
            bit = 2
            while bit < chan_count:
                early = early + flip(early, "chan", bit)
                bit *= 2
            own_m, resid_logits = early[:, :w_rows], early[:, w_rows:]
            pair_m = jnp.concatenate([own_m] + to_fast(own_m), axis=1)
            edges = xor_gather(after(edge, now), "chan", 2)
            extra = [pair_m, resid_logits] + feats + edges
        if k == 2:
            full = []
            for block in feats:
                full += [block, flip(block, "chan", 1)]
            feats, edges = full[:chan_count], full[chan_count:]
            part, part_edge = partial_products(
                [], feats, edges, shards[: 2 * fast], idx, group_at[:2], n_use
            )
            pair_m = after(pair_m, part)
            moved_m = [move_slow(pair_m, k) for k in range(1, slow)]
            extra = [pair_m, resid_logits, part, part_edge] + feats + edges + moved_m
        came, came_fast, extra = sync(came, came_fast, extra)
        now = came[0]
        shards += came_fast
        if k == 0:
            idx, edge, early = extra
        if k == 1:
            pair_m, resid_logits, *feats = extra
    pair_m, resid_logits, part, part_edge = extra[:4]
    moved_m = extra[4 + 2 * chan_count :]
    feats, edges = extra[4 : 4 + chan_count], extra[4 + chan_count : 4 + 2 * chan_count]
    shards.append(now)
    came_fast = to_fast(now)
    part, part_edge = partial_products(
        [part, part_edge], feats, edges, shards[2 * fast : 3 * fast], idx, group_at[2:3], n_use
    )
    feat_t = turned([after(feats[0], part)] + feats[1:])
    out_first = after(w_out, now)
    out_pair = jnp.stack([out_first, move_slow(out_first, 1)])
    out_third = move_slow(out_first, 3)
    per_chan = per_feat
    all_m = jnp.concatenate([pair_m] + moved_m, axis=1)
    pieces = [all_m[:, i * w_rows : (i + 1) * w_rows] for i in range(seq_count)]
    m_loc = jnp.concatenate(
        [picked(pieces, sources, chan * per_chan + i) for i in range(per_chan)], axis=1
    )
    head_scale = jnp.repeat(skip_d, HEADDIM)
    params = jnp.concatenate(
        [conv_weight, conv_bias[None], head_scale[None], norm_gain[None], norm_gain[None]], axis=0
    )
    came_fast, held = sync(came_fast, [now, out_pair, out_third, feat_t, part, m_loc, params])
    now, out_pair, out_third, feat_t, part, m_loc, params = held
    out_pair_fast = to_fast(out_pair)
    out_far = [move_slow(out_pair[1], 1), out_third]
    last = [now] + came_fast

    gate_pre, x_pre, x_edge, sums = front(
        part, part_edge, params, m_loc, feats, edges, last, idx, group_at[3:], n_use
    )
    sums = [sums] + [flip(sums, "chan", j) for j in range(1, chan_count)]
    out_far = jnp.stack([after(out_far[0], sums[0]), out_far[1]])
    out_far_fast = to_fast(out_far)
    loss_weight = 4.0 / math.sqrt(tok_rows * seq_count)
    dgate, dconv, normed, dlogit, mid, squares = back(
        gate_pre, x_pre, x_edge, params, m_loc, sums, resid_logits, targets[None], loss_weight
    )
    normed_x = xor_gather(normed, "chan", 2)
    future = shifted(dconv[:halo], -1)

    def far_grads(rhs, pair, vmem=16 * MIB):
        begin = n_idx // 2 + pair * (2 * fast - 2)
        return block_grads(feat_t, rhs, idx, begin, [2] * (fast - 1), w_rows, vmem)

    def near_grads(rhs):
        return block_grads(feat_t, rhs, idx, n_idx // 2 + len(far), [1] * slow, w_rows)

    def send_fast(blocks):
        return [move_fast(block, j) for j, block in enumerate(blocks, 1)]

    def total_of(own, came, i):
        return own[0].astype(f32) + sum(block[i].astype(f32) for block in came)

    def send_slow(own, came, i, k):
        return move_slow(total_of(own, came, i).astype(bf16), k)

    gate_first, held, out_pair_fast, out_far_fast = sync(
        far_grads(dgate, 0, PROJ_VMEM), [future, dconv, dlogit, dgate], out_pair_fast, out_far_fast
    )
    future, dconv, dlogit, dgate = held

    came = send_fast(gate_first)
    dpadded = jnp.concatenate([dconv, future], axis=0)
    dx_sum = jnp.zeros((tok_rows, local_inner), f32)
    for offset in range(KERNEL):
        dx_sum = (
            dx_sum + conv_weight[offset] * dpadded[halo - offset : halo - offset + tok_rows]
        )
    dx_pre = dx_sum.astype(bf16)
    gate_second = far_grads(dgate, 1)
    gate_own = near_grads(dgate)
    x_first = far_grads(dx_pre, 0)
    x_second = far_grads(dx_pre, 1)
    mid = after(mid, x_first[0], gate_own[0])
    mid_came = [move_slow(mid, k) for k in range(1, slow)]
    gate_first, gate_second, x_first, x_second, gate_own, normed_x, mid_came, held = sync(
        came, gate_second, x_first, x_second, gate_own, normed_x, mid_came, [dx_pre, mid]
    )
    dx_pre, mid = held
    mid = slow_total(mid, mid_came)

    came = send_fast(gate_second)
    gate_slow = [send_slow(gate_own[i], gate_first, i, first[i]) for i in range(2)]
    normed_all = []
    for block in normed_x:
        normed_all += [block, flip(block, "chan", 1)]
    out_shards = [out_pair] + out_pair_fast + [out_far] + out_far_fast
    counts = [[k * fast + j for k in ks] for ks in ((0, 1), (2, 3)) for j in range(fast)]
    raw = proj(normed_all, out_shards, counts, idx)
    x_own = near_grads(dx_pre)
    gate_second, gate_slow, x_first, x_second, x_own, held = sync(
        came, gate_slow, x_first, x_second, x_own, [raw]
    )
    raw = held[0]

    came = send_fast(x_first)
    gate_slow.append(send_slow(gate_own[2], gate_second, 0, second[0]))
    inv = lax.rsqrt(squares[0] / INNER + 1e-05)[:, None]
    new_resid = (resid.astype(f32) + inv * raw.astype(f32)).astype(bf16)
    head_local = lax.dot_general(
        dlogit, new_resid.astype(f32), (((1,), (0,)), ((), ())), precision=HI
    )
    mid_came = to_fast(mid)
    head_came = [move_slow(head_local, k) for k in range(1, slow)]
    x_first, x_second, x_own, gate_slow, mid_came, head_came, held = sync(
        came, x_second, x_own, gate_slow, mid_came, head_came, [mid, head_local]
    )
    mid, head_local = held
    mid = mid + sum(mid_came)
    head_local = slow_total(head_local, head_came)

    came = send_fast(x_second)
    x_terms = [total_of(x_own[i], x_first, i).astype(bf16) for i in range(2)]
    x_slow = [move_slow(x_terms[i], first[i]) for i in range(2)]
    head_came = to_fast(after(head_local, *x_terms))
    g_pieces = xor_gather(after(mid[:VOCAB], *x_terms), "chan")
    x_second, x_slow, head_came, g_pieces = sync(came, x_slow, head_came, g_pieces)

    x_slow.append(send_slow(x_own[2], x_second, 0, second[0]))
    head_local = head_local + sum(head_came)
    grad_gate_in = total_of(gate_own[3], gate_second, 1) + sum(
        block.astype(f32) for block in gate_slow
    )
    grad_x_in = total_of(x_own[3], x_second, 1) + sum(block.astype(f32) for block in x_slow)
    grad_head = head_local.T
    seq = lax.axis_index("seq")
    g_chan = picked(g_pieces, [chan ^ j for j in range(chan_count)], seq // per_chan)
    g_rows = lax.dynamic_slice_in_dim(g_chan, (seq % per_chan) * w_rows, w_rows, 1)
    grad_out = lax.dot_general(
        g_rows, w_head.T.astype(f32), (((0,), (0,)), ((), ())), precision=HI
    )
    tail = mid[VOCAB:]
    grad_skip = tail[KERNEL + 1].reshape(-1, HEADDIM).sum(axis=1)
    return (
        new_resid,
        grad_gate_in,
        grad_x_in,
        grad_out,
        grad_head,
        tail[:KERNEL],
        tail[KERNEL],
        grad_skip,
        tail[KERNEL + 2],
    )


def solution(mesh):
    return jax.shard_map(
        per_device,
        mesh=mesh,
        in_specs=(
            P("seq"),
            P("seq", "chan"),
            P("seq", "chan"),
            P("seq", "chan"),
            P(None, "chan"),
            P("chan"),
            P("chan"),
            P("chan"),
            P("seq", "chan"),
            P("chan", None),
        ),
        out_specs=(
            P("seq", "chan"),
            P("seq", "chan"),
            P("seq", "chan"),
            P("seq", "chan"),
            P("chan", None),
            P(None, "chan"),
            P("chan"),
            P("chan"),
            P("chan"),
        ),
        check_vma=False,
    )
```

```python
import functools
import math

import jax
import jax.numpy as jnp
from jax import lax
from jax.experimental import pallas as pl
from jax.experimental.pallas import tpu as pltpu
from jax.sharding import PartitionSpec as P

HEADDIM = 64
KERNEL = 4
VOCAB = 16
INNER = 2560
f32 = jnp.float32
bf16 = jnp.bfloat16
HI = lax.Precision.HIGHEST
EDGE = 16
LIGHT = pl.CostEstimate(flops=1, bytes_accessed=1, transcendentals=0)
MIB = 1024 * 1024
PROJ_VMEM = 58 * MIB


def slope(value, sig):
    return sig * (1.0 + value * (1.0 - sig))


def after(value, *others):
    return lax.optimization_barrier((value,) + others)[0]


def flip(value, axis, bit):
    return lax.ppermute(value, axis, [(i, i ^ bit) for i in range(lax.axis_size(axis))])


def xor_sum(value, axis):
    bit = 1
    while bit < lax.axis_size(axis):
        value = value + flip(value, axis, bit)
        bit *= 2
    return value


def xor_gather(value, axis, least=1):
    size = lax.axis_size(axis)
    blocks = {0: value}
    bit = size // 2
    while bit >= least:
        for j in list(blocks):
            blocks[j | bit] = flip(blocks[j], axis, bit)
        bit //= 2
    return [blocks[j] for j in range(0, size, least)]


def seq_factors():
    slow = 4
    return slow, lax.axis_size("seq") // slow


def move_slow(value, by):
    slow, fast = seq_factors()
    pairs = [(a * fast + b, ((a + by) % slow) * fast + b) for a in range(slow) for b in range(fast)]
    return lax.ppermute(value, "seq", pairs)


def move_fast(value, by):
    slow, fast = seq_factors()
    pairs = [(a * fast + b, a * fast + (b + by) % fast) for a in range(slow) for b in range(fast)]
    return lax.ppermute(value, "seq", pairs)


def shifted(array, by):
    length = lax.axis_size("seq")
    return lax.ppermute(array, "seq", [(i, i + by) for i in range(length) if 0 <= i + by < length])


def sync(*groups):
    flat = lax.optimization_barrier(tuple(value for group in groups for value in group))
    out, at = [], 0
    for group in groups:
        out.append(list(flat[at : at + len(group)]))
        at += len(group)
    return out


def to_fast(block):
    return [move_fast(block, j) for j in range(1, seq_factors()[1])]


def slow_total(own, came):
    even, odd = own + came[1], came[0] + came[2]
    return even + odd


def gather_sources():
    slow, fast = seq_factors()
    me = lax.axis_index("seq")
    a, b = me // fast, me % fast
    return [((a - k) % slow) * fast + (b - j) % fast for k in range(slow) for j in range(fast)]


def picked(pieces, sources, wanted):
    return sum(jnp.where(source == wanted, piece, 0.0) for source, piece in zip(sources, pieces))


def turn_kernel(n_feat, *refs):
    for j in range(n_feat):
        refs[n_feat][j] = refs[j][...].T


def turned(feats):
    tok, depth = feats[0].shape
    n_feat = len(feats)
    tile = 256
    return pl.pallas_call(
        functools.partial(turn_kernel, n_feat),
        out_shape=jax.ShapeDtypeStruct((n_feat, depth, tok), bf16),
        grid=(tok // tile,),
        in_specs=[pl.BlockSpec((tile, depth), lambda i: (i, 0))] * n_feat,
        out_specs=pl.BlockSpec((n_feat, depth, tile), lambda i: (0, 0, i)),
        compiler_params=pltpu.CompilerParams(vmem_limit_bytes=PROJ_VMEM),
        cost_estimate=LIGHT,
    )(*feats)


def proj_kernel(n_feat, counts, idx, *refs):
    feats = refs[:n_feat]
    shards = refs[n_feat : n_feat + len(counts)]
    out = refs[n_feat + len(counts)]
    fbuf, wbuf, fsem, wsem = refs[n_feat + len(counts) + 1 :]
    rows = shards[0].shape[1]
    tok, depth = feats[0].shape
    joined = len(fbuf.shape) == 2
    n_tile = fsem.shape[1]
    tile = tok // n_tile

    def f_copy(j, t):
        at = pl.ds(t * tile, tile)
        to = fbuf.at[at, pl.ds(j * depth, depth)] if joined else fbuf.at[j, at]
        return pltpu.make_async_copy(feats[j].at[at], to, fsem.at[j, t])

    copies = []
    for shard, places in zip(shards, counts):
        for i, s in enumerate(places):
            place = pl.ds(pl.multiple_of(idx[n_feat + s] * rows, 16), rows)
            copies.append(pltpu.make_async_copy(shard.at[i], wbuf.at[place], wsem.at[s]))
    for copy in copies:
        copy.start()
    for t in range(n_tile):
        for j in range(n_feat):
            f_copy(j, t).start()
    for copy in copies:
        copy.wait()
    for t in range(n_tile):
        at = pl.ds(t * tile, tile)
        for j in range(n_feat):
            f_copy(j, t).wait()
        if joined:
            total = jnp.dot(fbuf[at, :], wbuf[...], preferred_element_type=f32)
        else:
            total = jnp.zeros((tile, wbuf.shape[1]), f32)
            for j in range(n_feat):
                part = wbuf[j * depth : (j + 1) * depth, :]
                total += jnp.dot(fbuf[j, at, :], part, preferred_element_type=f32)
        out[at, :] = total.astype(out.dtype)


def proj(feats, shards, counts, idx):
    tok, depth = feats[0].shape
    rows, cols = shards[0].shape[1:]
    n_feat, n_shard = len(feats), sum(len(places) for places in counts)
    any_spec = pl.BlockSpec(memory_space=pltpu.HBM)
    return pl.pallas_call(
        functools.partial(proj_kernel, n_feat, counts),
        out_shape=jax.ShapeDtypeStruct((tok, cols), bf16),
        in_specs=[pl.BlockSpec(memory_space=pltpu.SMEM)] + [any_spec] * (n_feat + len(shards)),
        out_specs=pl.BlockSpec(memory_space=pltpu.VMEM),
        scratch_shapes=[
            pltpu.VMEM((tok, n_feat * depth) if depth % 128 == 0 else (n_feat, tok, depth), bf16),
            pltpu.VMEM((n_shard * rows, cols), bf16),
            pltpu.SemaphoreType.DMA((n_feat, 2)),
            pltpu.SemaphoreType.DMA((n_shard,)),
        ],
        compiler_params=pltpu.CompilerParams(vmem_limit_bytes=PROJ_VMEM),
        cost_estimate=LIGHT,
    )(idx, *feats, *shards)


def bring(n_feat, n_fast, n_use, ats, idx, feats, edges, shards, bufs):
    fbuf, ebuf, wbuf, fsem, esem, wsem = bufs
    rows = shards[0].shape[1]
    depth = feats[0].shape[1]
    blocks = range(n_use * len(ats))

    def slot(buf, m):
        return buf.at[:, pl.ds(m * depth, depth)] if len(buf.shape) == 2 else buf.at[m]

    def w_copy(i):
        at = ats[i // n_fast] + n_use + i % n_fast
        place = pl.multiple_of((i // n_fast * n_fast + idx[at]) * rows, 16)
        return pltpu.make_async_copy(shards[i], wbuf.at[:, pl.ds(place, rows)], wsem.at[i])

    for m in blocks:
        for j in range(n_feat):

            @pl.when(idx[ats[m // n_use] + m % n_use] == j)
            def _():
                pltpu.make_async_copy(feats[j], slot(fbuf, m), fsem.at[m]).start()
                pltpu.make_async_copy(edges[j], slot(ebuf, m), esem.at[m]).start()

    for i in range(len(shards)):
        w_copy(i).start()
    for i in range(len(shards)):
        w_copy(i).wait()
    for m in blocks:
        pltpu.make_async_copy(edges[0], slot(ebuf, m), esem.at[m]).wait()
        pltpu.make_async_copy(feats[0], slot(fbuf, m), fsem.at[m]).wait()


def product(buf, here, weights):
    if len(buf.shape) == 2:
        return jnp.dot(buf[here, :], weights[...], preferred_element_type=f32)
    depth = buf.shape[2]
    total = None
    for m in range(buf.shape[0]):
        rhs = weights[m * depth : (m + 1) * depth, :]
        term = jnp.dot(buf[m, here, :], rhs, preferred_element_type=f32)
        total = term if total is None else total + term
    return total


def part_kernel(n_feat, n_fast, n_use, ats, more, idx, *refs):
    if more:
        part, part_edge = refs[:2]
        refs = refs[2:]
    n_shard = n_fast * len(ats)
    feats, edges = refs[:n_feat], refs[n_feat : 2 * n_feat]
    shards = refs[2 * n_feat : 2 * n_feat + n_shard]
    out, out_edge = refs[2 * n_feat + n_shard : 2 * n_feat + n_shard + 2]
    bufs = refs[-6:]
    fbuf, ebuf, wbuf = bufs[:3]
    step = pl.program_id(0)
    tile = out.shape[1]

    @pl.when(step == 0)
    def _():
        bring(n_feat, n_fast, n_use, ats, idx, feats, edges, shards, bufs)
        term = product(ebuf, pl.ds(0, EDGE), wbuf.at[1])
        out_edge[...] = term + part_edge[...] if more else term

    here = pl.ds(pl.multiple_of(step * tile, tile), tile)
    for w in range(2):
        term = product(fbuf, here, wbuf.at[w])
        out[w] = term + part[w] if more else term


def front_kernel(n_feat, n_fast, n_use, ats, idx, part, part_edge, params, m_loc, *refs):
    n_shard = n_fast * len(ats)
    feats, edges = refs[:n_feat], refs[n_feat : 2 * n_feat]
    shards = refs[2 * n_feat : 2 * n_feat + n_shard]
    outs = refs[2 * n_feat + n_shard :]
    gate_out, x_out, normed_out, edge_out, z_out = outs[:5]
    xs, zs, ms = refs[-9:-6]
    bufs = refs[-6:]
    fbuf, ebuf, wbuf = bufs[:3]
    step = pl.program_id(0)
    tile = x_out.shape[0]

    @pl.when(step == 0)
    def _():
        bring(n_feat, n_fast, n_use, ats, idx, feats, edges, shards, bufs)
        edge = (part_edge[...] + product(ebuf, pl.ds(0, EDGE), wbuf.at[1])).astype(bf16)
        edge_out[...] = edge
        high, low = halves(m_loc[...])
        ms[...] = jnp.zeros_like(ms)
        ms[0:VOCAB, :] = high
        ms[VOCAB : 2 * VOCAB, :] = low
        xs[0:8, :] = edge.astype(f32)[EDGE - 8 :, :]

    @pl.when(step > 0)
    def _():
        xs[0:8, :] = xs[tile : tile + 8, :]

    here = pl.ds(pl.multiple_of(step * tile, tile), tile)
    x = (part[1] + product(fbuf, here, wbuf.at[1])).astype(bf16)
    x_out[...] = x
    xs[8 : 8 + tile, :] = x.astype(f32)
    gate = (part[0] + product(fbuf, here, wbuf.at[0])).astype(bf16)
    gate_out[...] = gate
    gate = gate.astype(f32)
    conv = params[4:5, :]
    for k in range(KERNEL):
        conv = conv + params[k : k + 1, :] * xs[5 + k : 5 + k + tile, :]
    gated = conv * jax.nn.sigmoid(conv) * params[5:6, :] * (gate * jax.nn.sigmoid(gate))
    normed = (gated * params[6:7, :]).astype(bf16)
    normed_out[...] = normed
    z = lax.dot_general(
        normed, ms[...], (((1,), (1,)), ((), ())), preferred_element_type=f32
    )
    square = jnp.sum(gated * gated, axis=1, keepdims=True)
    lane = lax.broadcasted_iota(jnp.int32, z.shape, 1)
    zs[here, :] = jnp.where(lane == 2 * VOCAB, square, z)

    @pl.when(step == pl.num_programs(0) - 1)
    def _():
        turned_z = zs[...].T
        z_out[0:VOCAB, :] = turned_z[0:VOCAB, :] + turned_z[VOCAB : 2 * VOCAB, :]
        z_out[VOCAB:, :] = turned_z[2 * VOCAB : 2 * VOCAB + 8, :]


def halves(value):
    high = value.astype(bf16)
    return high, (value - high.astype(f32)).astype(bf16)


def in_specs_of(feats, edges, shards):
    return [pl.BlockSpec(memory_space=pltpu.HBM)] * (len(feats) + len(edges) + len(shards))


def buffers_of(feats, shards, n_block):
    tok, depth = feats[0].shape
    count, rows, cols = shards[0].shape
    joined = depth % 128 == 0
    return [
        pltpu.VMEM((tok, n_block * depth) if joined else (n_block, tok, depth), bf16),
        pltpu.VMEM((EDGE, n_block * depth) if joined else (n_block, EDGE, depth), bf16),
        pltpu.VMEM((count, len(shards) * rows, cols), bf16),
        pltpu.SemaphoreType.DMA((n_block,)),
        pltpu.SemaphoreType.DMA((n_block,)),
        pltpu.SemaphoreType.DMA((len(shards),)),
    ]


def partial_products(parts, feats, edges, shards, idx, ats, n_use):
    count, rows, cols = shards[0].shape
    tok = feats[0].shape[0]
    n_fast = len(shards) // len(ats)
    tile = tok // 4
    part_specs = [
        pl.BlockSpec((count, tile, cols), lambda i, idx: (0, i, 0)),
        pl.BlockSpec((EDGE, cols), lambda i, idx: (0, 0)),
    ]
    return pl.pallas_call(
        functools.partial(part_kernel, len(feats), n_fast, n_use, ats, len(parts) > 0),
        out_shape=[
            jax.ShapeDtypeStruct((count, tok, cols), f32),
            jax.ShapeDtypeStruct((EDGE, cols), f32),
        ],
        grid_spec=pltpu.PrefetchScalarGridSpec(
            num_scalar_prefetch=1,
            grid=(tok // tile,),
            in_specs=part_specs[: len(parts)] + in_specs_of(feats, edges, shards),
            out_specs=part_specs,
            scratch_shapes=buffers_of(feats, shards, n_use * len(ats)),
        ),
        compiler_params=pltpu.CompilerParams(vmem_limit_bytes=PROJ_VMEM),
        cost_estimate=LIGHT,
    )(idx, *parts, *feats, *edges, *shards)


def front(part, part_edge, params, m_loc, feats, edges, shards, idx, ats, n_use):
    count, rows, cols = shards[0].shape
    tok = feats[0].shape[0]
    n_fast = len(shards) // len(ats)
    tile = tok // 4
    fixed = [pl.BlockSpec(a.shape, lambda i, idx: (0, 0)) for a in (part_edge, params, m_loc)]
    rows_spec = pl.BlockSpec((tile, cols), lambda i, idx: (i, 0))
    return pl.pallas_call(
        functools.partial(front_kernel, len(feats), n_fast, n_use, ats),
        out_shape=[
            jax.ShapeDtypeStruct((tok, cols), bf16),
            jax.ShapeDtypeStruct((tok, cols), bf16),
            jax.ShapeDtypeStruct((tok, cols), bf16),
            jax.ShapeDtypeStruct((EDGE, cols), bf16),
            jax.ShapeDtypeStruct((VOCAB + 8, tok), f32),
        ],
        grid_spec=pltpu.PrefetchScalarGridSpec(
            num_scalar_prefetch=1,
            grid=(tok // tile,),
            in_specs=[pl.BlockSpec((count, tile, cols), lambda i, idx: (0, i, 0))]
            + fixed
            + in_specs_of(feats, edges, shards),
            out_specs=[
                rows_spec,
                rows_spec,
                rows_spec,
                pl.BlockSpec((EDGE, cols), lambda i, idx: (0, 0)),
                pl.BlockSpec((VOCAB + 8, tok), lambda i, idx: (0, 0)),
            ],
            scratch_shapes=[
                pltpu.VMEM((tile + 8, cols), f32),
                pltpu.VMEM((tok, 128), f32),
                pltpu.VMEM((128, cols), bf16),
            ]
            + buffers_of(feats, shards, n_use * len(ats)),
        ),
        compiler_params=pltpu.CompilerParams(vmem_limit_bytes=PROJ_VMEM),
        cost_estimate=LIGHT,
    )(idx, part, part_edge, params, m_loc, *feats, *edges, *shards)


def back_kernel(
    weight, n_sum, gate_in, x_in, edge, params, m_loc, resid_logits, targets, *refs
):
    parts = refs[:n_sum]
    dgate_out, dconv_out, first_out, dlogit_out, acc, square_out, xs = refs[n_sum:]
    step = pl.program_id(0)
    tile = x_in.shape[0]

    @pl.when(step == 0)
    def _():
        acc[...] = jnp.zeros_like(acc)
        xs[0:8, :] = edge[...].astype(f32)[EDGE - 8 :, :]

    @pl.when(step > 0)
    def _():
        xs[0:8, :] = xs[tile : tile + 8, :]

    sums = parts[0][...]
    for other in parts[1:]:
        sums = sums + other[...]
    z = sums[0:VOCAB, :]
    square_out[...] = sums[VOCAB:, :]
    inverse = lax.rsqrt(sums[VOCAB : VOCAB + 1, :] / INNER + 1e-05)
    raised = jnp.exp(resid_logits[...] + inverse * z)
    probs = raised / jnp.sum(raised, axis=0, keepdims=True)
    row = lax.broadcasted_iota(jnp.int32, probs.shape, 0)
    onehot = jnp.where(row == targets[...], 1.0, 0.0)
    dlogit = (probs - onehot) * weight
    dlogit_out[...] = dlogit
    dot_gn = jnp.sum(dlogit * z, axis=0, keepdims=True)
    coef = inverse * inverse * inverse * dot_gn / INNER
    which = lax.broadcasted_iota(jnp.int32, (8, tile), 0)
    columns = jnp.where(which == 0, inverse, coef).T
    inv, coef = columns[:, 0:1], columns[:, 1:2]

    xs[8 : 8 + tile, :] = x_in[...].astype(f32)
    conv = params[4:5, :]
    for k in range(KERNEL):
        conv = conv + params[k : k + 1, :] * xs[5 + k : 5 + k + tile, :]
    scale, gain = params[5:6, :], params[6:7, :]
    sig_conv = jax.nn.sigmoid(conv)
    active = conv * sig_conv
    gate = gate_in[...].astype(f32)
    sig_gate = jax.nn.sigmoid(gate)
    silu_gate = gate * sig_gate
    gated = active * scale * silu_gate
    normed = gated * gain
    high, low = halves(dlogit)
    sums_out = jnp.dot(
        jnp.concatenate([high, low], axis=0),
        (normed * inv).astype(bf16),
        preferred_element_type=f32,
    )
    acc[0:VOCAB, :] += sums_out[0:VOCAB, :] + sums_out[VOCAB:, :]
    m_high, m_low = halves(m_loc[...])
    dnormed = lax.dot_general(
        jnp.concatenate([high, high, low], axis=0),
        jnp.concatenate([m_high, m_low, m_high], axis=0),
        (((0,), (0,)), ((), ())),
        preferred_element_type=f32,
    )
    scaled = dnormed * inv
    acc[VOCAB + 6 : VOCAB + 7, :] += jnp.sum(scaled * gated, axis=0, keepdims=True)
    dgated = scaled * gain - gated * coef
    both = dgated * active
    acc[VOCAB + 5 : VOCAB + 6, :] += jnp.sum(both * silu_gate, axis=0, keepdims=True)
    dgate_out[...] = (both * scale * slope(gate, sig_gate)).astype(bf16)
    dconv = dgated * scale * silu_gate * slope(conv, sig_conv)
    dconv_out[...] = dconv

    @pl.when(step == 0)
    def _():
        first_out[...] = dconv[0:8, :]

    acc[VOCAB + 4 : VOCAB + 5, :] += jnp.sum(dconv, axis=0, keepdims=True)
    for k in range(KERNEL):
        tap = jnp.sum(dconv * xs[5 + k : 5 + k + tile, :], axis=0, keepdims=True)
        acc[VOCAB + k : VOCAB + k + 1, :] += tap


def back(gate_pre, x_pre, edge, params, m_loc, sums, resid_logits, targets, weight):
    tok, cols = x_pre.shape
    tile = tok // 4
    rows_spec = pl.BlockSpec((tile, cols), lambda i: (i, 0))

    def fixed(a):
        return pl.BlockSpec(a.shape, lambda i: (0, 0))

    def tokens(a):
        return pl.BlockSpec((a.shape[0], tile), lambda i: (0, i))

    return pl.pallas_call(
        functools.partial(back_kernel, weight, len(sums)),
        out_shape=[
            jax.ShapeDtypeStruct((tok, cols), bf16),
            jax.ShapeDtypeStruct((tok, cols), f32),
            jax.ShapeDtypeStruct((8, cols), f32),
            jax.ShapeDtypeStruct((VOCAB, tok), f32),
            jax.ShapeDtypeStruct((VOCAB + 8, cols), f32),
            jax.ShapeDtypeStruct((8, tok), f32),
        ],
        grid=(tok // tile,),
        in_specs=[rows_spec, rows_spec, fixed(edge), fixed(params), fixed(m_loc)]
        + [tokens(a) for a in (resid_logits, targets, *sums)],
        out_specs=[
            rows_spec,
            rows_spec,
            pl.BlockSpec((8, cols), lambda i: (0, 0)),
            pl.BlockSpec((VOCAB, tile), lambda i: (0, i)),
            pl.BlockSpec((VOCAB + 8, cols), lambda i: (0, 0)),
            pl.BlockSpec((8, tile), lambda i: (0, i)),
        ],
        scratch_shapes=[pltpu.VMEM((tile + 8, cols), f32)],
        compiler_params=pltpu.CompilerParams(vmem_limit_bytes=PROJ_VMEM),
        cost_estimate=LIGHT,
    )(gate_pre, x_pre, edge, params, m_loc, resid_logits, targets, *sums)


def blocks_kernel(sizes, idx, lhs, rhs, *outs):
    at = 0
    for out, size in zip(outs, sizes):
        for i in range(size):

            @pl.when(pl.program_id(0) == at)
            def _():
                total = jnp.dot(lhs[0], rhs[...], preferred_element_type=f32)
                out[i] = total.astype(bf16)

            at += 1


def block_grads(feat_t, rhs, places, begin, sizes, rows, vmem=16 * MIB):
    tok = feat_t.shape[2]
    cols = rhs.shape[1]

    def place(i, idx):
        return (idx[2 * (begin + i)], idx[2 * (begin + i) + 1], 0)

    return pl.pallas_call(
        functools.partial(blocks_kernel, sizes),
        out_shape=[jax.ShapeDtypeStruct((size, rows, cols), bf16) for size in sizes],
        grid_spec=pltpu.PrefetchScalarGridSpec(
            num_scalar_prefetch=1,
            grid=(sum(sizes),),
            in_specs=[
                pl.BlockSpec((1, rows, tok), place),
                pl.BlockSpec((tok, cols), lambda i, idx: (0, 0)),
            ],
            out_specs=[
                pl.BlockSpec((size, rows, cols), lambda i, idx: (0, 0, 0)) for size in sizes
            ],
        ),
        compiler_params=pltpu.CompilerParams(vmem_limit_bytes=vmem),
        cost_estimate=LIGHT,
    )(places, feat_t, rhs)


def dest_places(keys, rows, depth):
    slow, fast = seq_factors()
    me = lax.axis_index("seq")
    per_feat = depth // rows
    out = []
    for k, j in keys:
        dest = ((me // fast + k) % slow) * fast + (me % fast + j) % fast
        out += [(dest // per_feat) ^ lax.axis_index("chan"), dest % per_feat]
    return out


def slow_order():
    return [2, 3, 1, 0]


def per_device(
    targets, resid, w_gate_in, w_x_in, conv_weight, conv_bias, skip_d, norm_gain, w_out, w_head
):
    tok_rows = resid.shape[0]
    seq_count = lax.axis_size("seq")
    chan_count = lax.axis_size("chan")
    chan = lax.axis_index("chan")
    local_inner = w_gate_in.shape[1]
    w_rows = w_out.shape[0]
    halo = KERNEL - 1

    sources = gather_sources()
    slow, fast = seq_factors()
    order = slow_order()
    first, second = order[:2], order[2:]
    far = [(k, j) for pair in (first, second) for j in range(1, fast) for k in pair]
    near = [(k, 0) for k in order]
    per_feat = resid.shape[1] // w_rows
    idx = [chan ^ j for j in range(chan_count)]
    idx += [((i // per_feat) ^ chan) * per_feat + i % per_feat for i in sources]
    idx += dest_places(far + near, w_rows, resid.shape[1])
    n_idx = chan_count + seq_count
    n_use = fast // per_feat
    group_at = []
    for k in range(slow):
        group_at.append(len(idx))
        mine = sources[k * fast : (k + 1) * fast]
        idx += [(mine[0] // fast * n_use + m) ^ chan for m in range(n_use)]
        idx += [source % fast for source in mine]
    idx = jnp.concatenate([jnp.reshape(i, (1,)) for i in idx]).astype(jnp.int32)

    now = jnp.stack([w_gate_in, w_x_in])
    shards = []
    extra = [idx]
    for k in range(slow - 1):
        shards.append(now)
        came = [move_slow(now, 1)]
        came_fast = to_fast(now)
        if k == 0:
            feats = xor_gather(resid, "chan", 2)
            edge = shifted(resid[tok_rows - EDGE :], 1)
            head_t = w_head.T
            part_m = lax.dot_general(
                head_t, w_out, (((1,), (1,)), ((), ())), preferred_element_type=f32
            )
            part_r = lax.dot_general(
                head_t, resid, (((1,), (1,)), ((), ())), preferred_element_type=f32
            )
            early = jnp.concatenate([part_m, part_r], axis=1)
            early = early + flip(early, "chan", 1)
            head_scale = jnp.repeat(skip_d, HEADDIM)
            params = [conv_weight, conv_bias[None], head_scale[None]] + [norm_gain[None]] * 2
            params = jnp.concatenate(params, axis=0)
            extra = [idx, edge, early, params]
        if k == 1:
            bit = 2
            while bit < chan_count:
                early = early + flip(early, "chan", bit)
                bit *= 2
            own_m, resid_logits = early[:, :w_rows], early[:, w_rows:]
            pair_m = jnp.concatenate([own_m] + to_fast(own_m), axis=1)
            edges = xor_gather(after(edge, now), "chan", 2)
            extra = [pair_m, resid_logits] + feats + edges
        if k == 2:
            full = []
            for block in feats:
                full += [block, flip(block, "chan", 1)]
            feats, edges = full[:chan_count], full[chan_count:]
            part, part_edge = partial_products(
                [], feats, edges, shards[: 2 * fast], idx, group_at[:2], n_use
            )
            pair_m = after(pair_m, part)
            moved_m = [move_slow(pair_m, k) for k in range(1, slow)]
            extra = [pair_m, resid_logits, part, part_edge] + feats + edges
        came, came_fast, extra = sync(came, came_fast, extra)
        now = came[0]
        shards += came_fast
        if k == 0:
            idx, edge, early, params = extra
        if k == 1:
            pair_m, resid_logits, *feats = extra
    pair_m, resid_logits, part, part_edge = extra[:4]
    feats, edges = extra[4 : 4 + chan_count], extra[4 + chan_count : 4 + 2 * chan_count]
    shards.append(now)
    came_fast = to_fast(now)
    part, part_edge = partial_products(
        [part, part_edge], feats, edges, shards[2 * fast : 3 * fast], idx, group_at[2:3], n_use
    )
    feat_t = turned([after(feats[0], part)] + feats[1:])
    out_first = after(w_out, now)
    out_pair = jnp.stack([out_first, move_slow(out_first, 1)])
    out_third = move_slow(out_first, 3)
    per_chan = per_feat
    all_m = jnp.concatenate([pair_m] + moved_m, axis=1)
    pieces = [all_m[:, i * w_rows : (i + 1) * w_rows] for i in range(seq_count)]
    m_loc = jnp.concatenate(
        [picked(pieces, sources, chan * per_chan + i) for i in range(per_chan)], axis=1
    )
    came_fast, held = sync(came_fast, [now, out_pair, feat_t, part, m_loc])
    now, out_pair, feat_t, part, m_loc = held
    out_pair_fast = to_fast(out_pair)
    out_far = [move_slow(out_pair[1], 1), out_third]
    last = [now] + came_fast

    gate_pre, x_pre, normed, x_edge, sums = front(
        part, part_edge, params, m_loc, feats, edges, last, idx, group_at[3:], n_use
    )
    sums = [sums] + [flip(sums, "chan", j) for j in range(1, chan_count)]
    out_far = jnp.stack([after(out_far[0], sums[0]), out_far[1]])
    out_far_fast = to_fast(out_far)
    loss_weight = 4.0 / math.sqrt(tok_rows * seq_count)
    normed_x = xor_gather(after(normed, *sums[1:]), "chan", 2)
    dgate, dconv, dfirst, dlogit, mid, squares = back(
        gate_pre, x_pre, x_edge, params, m_loc, sums, resid_logits, targets[None], loss_weight
    )
    future = shifted(dfirst, -1)[:halo]

    def far_grads(rhs, pair, vmem=16 * MIB):
        begin = n_idx // 2 + pair * (2 * fast - 2)
        return block_grads(feat_t, rhs, idx, begin, [2] * (fast - 1), w_rows, vmem)

    def near_grads(rhs):
        return block_grads(feat_t, rhs, idx, n_idx // 2 + len(far), [1] * slow, w_rows)

    def send_fast(blocks):
        return [move_fast(block, j) for j, block in enumerate(blocks, 1)]

    def total_of(own, came, i):
        return own[0].astype(f32) + sum(block[i].astype(f32) for block in came)

    hops = [1, 3]

    gate_first, held, out_pair_fast, out_far_fast = sync(
        far_grads(dgate, 0, PROJ_VMEM), [future, dconv, dlogit, dgate], out_pair_fast, out_far_fast
    )
    future, dconv, dlogit, dgate = held

    came = send_fast(gate_first)
    dpadded = jnp.concatenate([dconv, future], axis=0)
    dx_sum = jnp.zeros((tok_rows, local_inner), f32)
    for offset in range(KERNEL):
        dx_sum = (
            dx_sum + conv_weight[offset] * dpadded[halo - offset : halo - offset + tok_rows]
        )
    dx_pre = dx_sum.astype(bf16)
    gate_second = far_grads(dgate, 1)
    gate_own = near_grads(dgate)
    x_first = far_grads(dx_pre, 0)
    x_second = far_grads(dx_pre, 1)
    mid = after(mid, x_first[0], gate_own[0])
    mid_came = [move_slow(mid, k) for k in range(1, slow)]
    gate_first, gate_second, x_first, x_second, gate_own, normed_x, mid_came, held = sync(
        came, gate_second, x_first, x_second, gate_own, normed_x, mid_came, [dx_pre, mid]
    )
    dx_pre, mid = held
    mid = slow_total(mid, mid_came)

    came = send_fast(gate_second)
    gate_terms = [total_of(gate_own[i], gate_first, i).astype(bf16) for i in range(2)]
    gate_slow = [move_slow(term, by) for term, by in zip(gate_terms, hops)]
    normed_all = []
    for block in normed_x:
        normed_all += [block, flip(block, "chan", 1)]
    out_shards = [out_pair] + out_pair_fast + [out_far] + out_far_fast
    counts = [[k * fast + j for k in ks] for ks in ((0, 1), (2, 3)) for j in range(fast)]
    raw = proj(normed_all, out_shards, counts, idx)
    gate_second, gate_slow, x_first, x_second, held = sync(
        came, gate_slow, x_first, x_second, [raw, dx_pre]
    )
    raw, dx_pre = held

    came = send_fast(x_first)
    term = total_of(gate_own[2], gate_second, 0) + gate_slow[0].astype(f32)
    gate_slow[0] = move_slow(term.astype(bf16), 1)
    inv = lax.rsqrt(squares[0] / INNER + 1e-05)[:, None]
    new_resid = (resid.astype(f32) + inv * raw.astype(f32)).astype(bf16)
    head_local = lax.dot_general(
        dlogit, new_resid.astype(f32), (((1,), (0,)), ((), ())), precision=HI
    )
    x_own = near_grads(dx_pre)
    mid_came = to_fast(mid)
    head_local = after(head_local, x_own[0])
    head_came = [move_slow(head_local, k) for k in range(1, slow)]
    x_first, x_second, x_own, gate_slow, mid_came, head_came, held = sync(
        came, x_second, x_own, gate_slow, mid_came, head_came, [mid, head_local]
    )
    mid, head_local = held
    mid = mid + sum(mid_came)
    head_local = slow_total(head_local, head_came)

    came = send_fast(x_second)
    x_terms = [total_of(x_own[i], x_first, i).astype(bf16) for i in range(2)]
    x_slow = [move_slow(term, by) for term, by in zip(x_terms, hops)]
    head_came = to_fast(after(head_local, *x_terms))
    g_pieces = xor_gather(after(mid[:VOCAB], *x_terms), "chan")
    x_second, x_slow, head_came, g_pieces = sync(came, x_slow, head_came, g_pieces)

    term = total_of(x_own[2], x_second, 0) + x_slow[0].astype(f32)
    x_slow[0] = move_slow(term.astype(bf16), 1)
    head_local = head_local + sum(head_came)
    grad_gate_in = total_of(gate_own[3], gate_second, 1) + sum(
        block.astype(f32) for block in gate_slow
    )
    grad_x_in = total_of(x_own[3], x_second, 1) + sum(block.astype(f32) for block in x_slow)
    grad_head = head_local.T
    seq = lax.axis_index("seq")
    g_chan = picked(g_pieces, [chan ^ j for j in range(chan_count)], seq // per_chan)
    g_rows = lax.dynamic_slice_in_dim(g_chan, (seq % per_chan) * w_rows, w_rows, 1)
    grad_out = lax.dot_general(
        g_rows, w_head.T.astype(f32), (((0,), (0,)), ((), ())), precision=HI
    )
    tail = mid[VOCAB:]
    grad_skip = tail[KERNEL + 1].reshape(-1, HEADDIM).sum(axis=1)
    return (
        new_resid,
        grad_gate_in,
        grad_x_in,
        grad_out,
        grad_head,
        tail[:KERNEL],
        tail[KERNEL],
        grad_skip,
        tail[KERNEL + 2],
    )


def solution(mesh):
    return jax.shard_map(
        per_device,
        mesh=mesh,
        in_specs=(
            P("seq"),
            P("seq", "chan"),
            P("seq", "chan"),
            P("seq", "chan"),
            P(None, "chan"),
            P("chan"),
            P("chan"),
            P("chan"),
            P("seq", "chan"),
            P("chan", None),
        ),
        out_specs=(
            P("seq", "chan"),
            P("seq", "chan"),
            P("seq", "chan"),
            P("seq", "chan"),
            P("chan", None),
            P(None, "chan"),
            P("chan"),
            P("chan"),
            P("chan"),
        ),
        check_vma=False,
    )
```

```python
import functools
import math

import jax
import jax.numpy as jnp
from jax import lax
from jax.experimental import pallas as pl
from jax.experimental.pallas import tpu as pltpu
from jax.sharding import PartitionSpec as P

HEADDIM = 64
KERNEL = 4
VOCAB = 16
INNER = 2560
f32 = jnp.float32
bf16 = jnp.bfloat16
HI = lax.Precision.HIGHEST
EDGE = 16
LIGHT = pl.CostEstimate(flops=1, bytes_accessed=1, transcendentals=0)
MIB = 1024 * 1024
PROJ_VMEM = 58 * MIB


def slope(value, sig):
    return sig * (1.0 + value * (1.0 - sig))


def after(value, *others):
    return lax.optimization_barrier((value,) + others)[0]


def flip(value, axis, bit):
    return lax.ppermute(value, axis, [(i, i ^ bit) for i in range(lax.axis_size(axis))])


def xor_sum(value, axis):
    bit = 1
    while bit < lax.axis_size(axis):
        value = value + flip(value, axis, bit)
        bit *= 2
    return value


def xor_gather(value, axis, least=1):
    size = lax.axis_size(axis)
    blocks = {0: value}
    bit = size // 2
    while bit >= least:
        for j in list(blocks):
            blocks[j | bit] = flip(blocks[j], axis, bit)
        bit //= 2
    return [blocks[j] for j in range(0, size, least)]


def seq_factors():
    slow = 4
    return slow, lax.axis_size("seq") // slow


def move_slow(value, by):
    slow, fast = seq_factors()
    pairs = [(a * fast + b, ((a + by) % slow) * fast + b) for a in range(slow) for b in range(fast)]
    return lax.ppermute(value, "seq", pairs)


def move_fast(value, by):
    slow, fast = seq_factors()
    pairs = [(a * fast + b, a * fast + (b + by) % fast) for a in range(slow) for b in range(fast)]
    return lax.ppermute(value, "seq", pairs)


def shifted(array, by):
    length = lax.axis_size("seq")
    return lax.ppermute(array, "seq", [(i, i + by) for i in range(length) if 0 <= i + by < length])


def sync(*groups):
    flat = lax.optimization_barrier(tuple(value for group in groups for value in group))
    out, at = [], 0
    for group in groups:
        out.append(list(flat[at : at + len(group)]))
        at += len(group)
    return out


def to_fast(block):
    return [move_fast(block, j) for j in range(1, seq_factors()[1])]


def slow_total(own, came):
    even, odd = own + came[1], came[0] + came[2]
    return even + odd


def gather_sources():
    slow, fast = seq_factors()
    me = lax.axis_index("seq")
    a, b = me // fast, me % fast
    return [((a - k) % slow) * fast + (b - j) % fast for k in range(slow) for j in range(fast)]


def picked(pieces, sources, wanted):
    return sum(jnp.where(source == wanted, piece, 0.0) for source, piece in zip(sources, pieces))


def turn_kernel(n_feat, *refs):
    for j in range(n_feat):
        refs[n_feat][j] = refs[j][...].T


def turned(feats):
    tok, depth = feats[0].shape
    n_feat = len(feats)
    tile = 256
    return pl.pallas_call(
        functools.partial(turn_kernel, n_feat),
        out_shape=jax.ShapeDtypeStruct((n_feat, depth, tok), bf16),
        grid=(tok // tile,),
        in_specs=[pl.BlockSpec((tile, depth), lambda i: (i, 0))] * n_feat,
        out_specs=pl.BlockSpec((n_feat, depth, tile), lambda i: (0, 0, i)),
        compiler_params=pltpu.CompilerParams(vmem_limit_bytes=PROJ_VMEM),
        cost_estimate=LIGHT,
    )(*feats)


def proj_kernel(n_feat, counts, idx, *refs):
    feats = refs[:n_feat]
    shards = refs[n_feat : n_feat + len(counts)]
    out = refs[n_feat + len(counts)]
    fbuf, wbuf, fsem, wsem = refs[n_feat + len(counts) + 1 :]
    rows = shards[0].shape[1]
    tok, depth = feats[0].shape
    joined = len(fbuf.shape) == 2
    n_tile = fsem.shape[1]
    tile = tok // n_tile

    def f_copy(j, t):
        at = pl.ds(t * tile, tile)
        to = fbuf.at[at, pl.ds(j * depth, depth)] if joined else fbuf.at[j, at]
        return pltpu.make_async_copy(feats[j].at[at], to, fsem.at[j, t])

    copies = []
    for shard, places in zip(shards, counts):
        for i, s in enumerate(places):
            place = pl.ds(pl.multiple_of(idx[n_feat + s] * rows, 16), rows)
            copies.append(pltpu.make_async_copy(shard.at[i], wbuf.at[place], wsem.at[s]))
    for copy in copies:
        copy.start()
    for t in range(n_tile):
        for j in range(n_feat):
            f_copy(j, t).start()
    for copy in copies:
        copy.wait()
    for t in range(n_tile):
        at = pl.ds(t * tile, tile)
        for j in range(n_feat):
            f_copy(j, t).wait()
        if joined:
            total = jnp.dot(fbuf[at, :], wbuf[...], preferred_element_type=f32)
        else:
            total = jnp.zeros((tile, wbuf.shape[1]), f32)
            for j in range(n_feat):
                part = wbuf[j * depth : (j + 1) * depth, :]
                total += jnp.dot(fbuf[j, at, :], part, preferred_element_type=f32)
        out[at, :] = total.astype(out.dtype)


def proj(feats, shards, counts, idx):
    tok, depth = feats[0].shape
    rows, cols = shards[0].shape[1:]
    n_feat, n_shard = len(feats), sum(len(places) for places in counts)
    any_spec = pl.BlockSpec(memory_space=pltpu.HBM)
    return pl.pallas_call(
        functools.partial(proj_kernel, n_feat, counts),
        out_shape=jax.ShapeDtypeStruct((tok, cols), bf16),
        in_specs=[pl.BlockSpec(memory_space=pltpu.SMEM)] + [any_spec] * (n_feat + len(shards)),
        out_specs=pl.BlockSpec(memory_space=pltpu.VMEM),
        scratch_shapes=[
            pltpu.VMEM((tok, n_feat * depth) if depth % 128 == 0 else (n_feat, tok, depth), bf16),
            pltpu.VMEM((n_shard * rows, cols), bf16),
            pltpu.SemaphoreType.DMA((n_feat, 2)),
            pltpu.SemaphoreType.DMA((n_shard,)),
        ],
        compiler_params=pltpu.CompilerParams(vmem_limit_bytes=PROJ_VMEM),
        cost_estimate=LIGHT,
    )(idx, *feats, *shards)


def bring(n_feat, n_fast, n_use, ats, idx, feats, edges, shards, bufs):
    fbuf, ebuf, wbuf, fsem, esem, wsem = bufs
    rows = shards[0].shape[1]
    depth = feats[0].shape[1]
    blocks = range(n_use * len(ats))

    def slot(buf, m):
        return buf.at[:, pl.ds(m * depth, depth)] if len(buf.shape) == 2 else buf.at[m]

    def w_copy(i):
        at = ats[i // n_fast] + n_use + i % n_fast
        place = pl.multiple_of((i // n_fast * n_fast + idx[at]) * rows, 16)
        return pltpu.make_async_copy(shards[i], wbuf.at[:, pl.ds(place, rows)], wsem.at[i])

    for m in blocks:
        for j in range(n_feat):

            @pl.when(idx[ats[m // n_use] + m % n_use] == j)
            def _():
                pltpu.make_async_copy(feats[j], slot(fbuf, m), fsem.at[m]).start()
                pltpu.make_async_copy(edges[j], slot(ebuf, m), esem.at[m]).start()

    for i in range(len(shards)):
        w_copy(i).start()
    for i in range(len(shards)):
        w_copy(i).wait()
    for m in blocks:
        pltpu.make_async_copy(edges[0], slot(ebuf, m), esem.at[m]).wait()
        pltpu.make_async_copy(feats[0], slot(fbuf, m), fsem.at[m]).wait()


def product(buf, here, weights):
    if len(buf.shape) == 2:
        return jnp.dot(buf[here, :], weights[...], preferred_element_type=f32)
    depth = buf.shape[2]
    total = None
    for m in range(buf.shape[0]):
        rhs = weights[m * depth : (m + 1) * depth, :]
        term = jnp.dot(buf[m, here, :], rhs, preferred_element_type=f32)
        total = term if total is None else total + term
    return total


def part_kernel(n_feat, n_fast, n_use, ats, more, idx, *refs):
    if more:
        part, part_edge = refs[:2]
        refs = refs[2:]
    n_shard = n_fast * len(ats)
    feats, edges = refs[:n_feat], refs[n_feat : 2 * n_feat]
    shards = refs[2 * n_feat : 2 * n_feat + n_shard]
    out, out_edge = refs[2 * n_feat + n_shard : 2 * n_feat + n_shard + 2]
    bufs = refs[-6:]
    fbuf, ebuf, wbuf = bufs[:3]
    step = pl.program_id(0)
    tile = out.shape[1]

    @pl.when(step == 0)
    def _():
        bring(n_feat, n_fast, n_use, ats, idx, feats, edges, shards, bufs)
        term = product(ebuf, pl.ds(0, EDGE), wbuf.at[1])
        out_edge[...] = term + part_edge[...] if more else term

    here = pl.ds(pl.multiple_of(step * tile, tile), tile)
    for w in range(2):
        term = product(fbuf, here, wbuf.at[w])
        out[w] = term + part[w] if more else term


def front_kernel(n_feat, n_fast, n_use, ats, idx, part, part_edge, params, m_loc, *refs):
    n_shard = n_fast * len(ats)
    feats, edges = refs[:n_feat], refs[n_feat : 2 * n_feat]
    shards = refs[2 * n_feat : 2 * n_feat + n_shard]
    outs = refs[2 * n_feat + n_shard :]
    gate_out, x_out, normed_out, edge_out, z_out = outs[:5]
    xs, zs, ms = refs[-9:-6]
    bufs = refs[-6:]
    fbuf, ebuf, wbuf = bufs[:3]
    step = pl.program_id(0)
    tile = x_out.shape[0]

    @pl.when(step == 0)
    def _():
        bring(n_feat, n_fast, n_use, ats, idx, feats, edges, shards, bufs)
        edge = (part_edge[...] + product(ebuf, pl.ds(0, EDGE), wbuf.at[1])).astype(bf16)
        edge_out[...] = edge
        high, low = halves(m_loc[...])
        ms[...] = jnp.zeros_like(ms)
        ms[0:VOCAB, :] = high
        ms[VOCAB : 2 * VOCAB, :] = low
        xs[0:8, :] = edge.astype(f32)[EDGE - 8 :, :]

    @pl.when(step > 0)
    def _():
        xs[0:8, :] = xs[tile : tile + 8, :]

    here = pl.ds(pl.multiple_of(step * tile, tile), tile)
    x = (part[1] + product(fbuf, here, wbuf.at[1])).astype(bf16)
    x_out[...] = x
    xs[8 : 8 + tile, :] = x.astype(f32)
    gate = (part[0] + product(fbuf, here, wbuf.at[0])).astype(bf16)
    gate_out[...] = gate
    gate = gate.astype(f32)
    conv = params[4:5, :]
    for k in range(KERNEL):
        conv = conv + params[k : k + 1, :] * xs[5 + k : 5 + k + tile, :]
    gated = conv * jax.nn.sigmoid(conv) * params[5:6, :] * (gate * jax.nn.sigmoid(gate))
    normed = (gated * params[6:7, :]).astype(bf16)
    normed_out[...] = normed
    z = lax.dot_general(
        normed, ms[...], (((1,), (1,)), ((), ())), preferred_element_type=f32
    )
    square = jnp.sum(gated * gated, axis=1, keepdims=True)
    lane = lax.broadcasted_iota(jnp.int32, z.shape, 1)
    zs[here, :] = jnp.where(lane == 2 * VOCAB, square, z)

    @pl.when(step == pl.num_programs(0) - 1)
    def _():
        turned_z = zs[...].T
        z_out[0:VOCAB, :] = turned_z[0:VOCAB, :] + turned_z[VOCAB : 2 * VOCAB, :]
        z_out[VOCAB:, :] = turned_z[2 * VOCAB : 2 * VOCAB + 8, :]


def halves(value):
    high = value.astype(bf16)
    return high, (value - high.astype(f32)).astype(bf16)


def in_specs_of(feats, edges, shards):
    return [pl.BlockSpec(memory_space=pltpu.HBM)] * (len(feats) + len(edges) + len(shards))


def buffers_of(feats, shards, n_block):
    tok, depth = feats[0].shape
    count, rows, cols = shards[0].shape
    joined = depth % 128 == 0
    return [
        pltpu.VMEM((tok, n_block * depth) if joined else (n_block, tok, depth), bf16),
        pltpu.VMEM((EDGE, n_block * depth) if joined else (n_block, EDGE, depth), bf16),
        pltpu.VMEM((count, len(shards) * rows, cols), bf16),
        pltpu.SemaphoreType.DMA((n_block,)),
        pltpu.SemaphoreType.DMA((n_block,)),
        pltpu.SemaphoreType.DMA((len(shards),)),
    ]


def partial_products(parts, feats, edges, shards, idx, ats, n_use):
    count, rows, cols = shards[0].shape
    tok = feats[0].shape[0]
    n_fast = len(shards) // len(ats)
    tile = tok // 4
    part_specs = [
        pl.BlockSpec((count, tile, cols), lambda i, idx: (0, i, 0)),
        pl.BlockSpec((EDGE, cols), lambda i, idx: (0, 0)),
    ]
    return pl.pallas_call(
        functools.partial(part_kernel, len(feats), n_fast, n_use, ats, len(parts) > 0),
        out_shape=[
            jax.ShapeDtypeStruct((count, tok, cols), f32),
            jax.ShapeDtypeStruct((EDGE, cols), f32),
        ],
        grid_spec=pltpu.PrefetchScalarGridSpec(
            num_scalar_prefetch=1,
            grid=(tok // tile,),
            in_specs=part_specs[: len(parts)] + in_specs_of(feats, edges, shards),
            out_specs=part_specs,
            scratch_shapes=buffers_of(feats, shards, n_use * len(ats)),
        ),
        compiler_params=pltpu.CompilerParams(vmem_limit_bytes=PROJ_VMEM),
        cost_estimate=LIGHT,
    )(idx, *parts, *feats, *edges, *shards)


def front(part, part_edge, params, m_loc, feats, edges, shards, idx, ats, n_use):
    count, rows, cols = shards[0].shape
    tok = feats[0].shape[0]
    n_fast = len(shards) // len(ats)
    tile = tok // 4
    fixed = [pl.BlockSpec(a.shape, lambda i, idx: (0, 0)) for a in (part_edge, params, m_loc)]
    rows_spec = pl.BlockSpec((tile, cols), lambda i, idx: (i, 0))
    return pl.pallas_call(
        functools.partial(front_kernel, len(feats), n_fast, n_use, ats),
        out_shape=[
            jax.ShapeDtypeStruct((tok, cols), bf16),
            jax.ShapeDtypeStruct((tok, cols), bf16),
            jax.ShapeDtypeStruct((tok, cols), bf16),
            jax.ShapeDtypeStruct((EDGE, cols), bf16),
            jax.ShapeDtypeStruct((VOCAB + 8, tok), f32),
        ],
        grid_spec=pltpu.PrefetchScalarGridSpec(
            num_scalar_prefetch=1,
            grid=(tok // tile,),
            in_specs=[pl.BlockSpec((count, tile, cols), lambda i, idx: (0, i, 0))]
            + fixed
            + in_specs_of(feats, edges, shards),
            out_specs=[
                rows_spec,
                rows_spec,
                rows_spec,
                pl.BlockSpec((EDGE, cols), lambda i, idx: (0, 0)),
                pl.BlockSpec((VOCAB + 8, tok), lambda i, idx: (0, 0)),
            ],
            scratch_shapes=[
                pltpu.VMEM((tile + 8, cols), f32),
                pltpu.VMEM((tok, 128), f32),
                pltpu.VMEM((128, cols), bf16),
            ]
            + buffers_of(feats, shards, n_use * len(ats)),
        ),
        compiler_params=pltpu.CompilerParams(vmem_limit_bytes=PROJ_VMEM),
        cost_estimate=LIGHT,
    )(idx, part, part_edge, params, m_loc, *feats, *edges, *shards)


def back_kernel(
    weight, n_sum, gate_in, x_in, edge, params, m_loc, resid_logits, targets, *refs
):
    parts = refs[:n_sum]
    dgate_out, dconv_out, first_out, dlogit_out, acc, square_out, xs = refs[n_sum:]
    step = pl.program_id(0)
    tile = x_in.shape[0]

    @pl.when(step == 0)
    def _():
        acc[...] = jnp.zeros_like(acc)
        xs[0:8, :] = edge[...].astype(f32)[EDGE - 8 :, :]

    @pl.when(step > 0)
    def _():
        xs[0:8, :] = xs[tile : tile + 8, :]

    sums = parts[0][...]
    for other in parts[1:]:
        sums = sums + other[...]
    z = sums[0:VOCAB, :]
    square_out[...] = sums[VOCAB:, :]
    inverse = lax.rsqrt(sums[VOCAB : VOCAB + 1, :] / INNER + 1e-05)
    raised = jnp.exp(resid_logits[...] + inverse * z)
    probs = raised / jnp.sum(raised, axis=0, keepdims=True)
    row = lax.broadcasted_iota(jnp.int32, probs.shape, 0)
    onehot = jnp.where(row == targets[...], 1.0, 0.0)
    dlogit = (probs - onehot) * weight
    dlogit_out[...] = dlogit
    dot_gn = jnp.sum(dlogit * z, axis=0, keepdims=True)
    coef = inverse * inverse * inverse * dot_gn / INNER
    which = lax.broadcasted_iota(jnp.int32, (8, tile), 0)
    columns = jnp.where(which == 0, inverse, coef).T
    inv, coef = columns[:, 0:1], columns[:, 1:2]

    xs[8 : 8 + tile, :] = x_in[...].astype(f32)
    conv = params[4:5, :]
    for k in range(KERNEL):
        conv = conv + params[k : k + 1, :] * xs[5 + k : 5 + k + tile, :]
    scale, gain = params[5:6, :], params[6:7, :]
    sig_conv = jax.nn.sigmoid(conv)
    active = conv * sig_conv
    gate = gate_in[...].astype(f32)
    sig_gate = jax.nn.sigmoid(gate)
    silu_gate = gate * sig_gate
    gated = active * scale * silu_gate
    normed = gated * gain
    high, low = halves(dlogit)
    sums_out = jnp.dot(
        jnp.concatenate([high, low], axis=0),
        (normed * inv).astype(bf16),
        preferred_element_type=f32,
    )
    acc[0:VOCAB, :] += sums_out[0:VOCAB, :] + sums_out[VOCAB:, :]
    m_high, m_low = halves(m_loc[...])
    dnormed = lax.dot_general(
        jnp.concatenate([high, high, low], axis=0),
        jnp.concatenate([m_high, m_low, m_high], axis=0),
        (((0,), (0,)), ((), ())),
        preferred_element_type=f32,
    )
    scaled = dnormed * inv
    acc[VOCAB + 6 : VOCAB + 7, :] += jnp.sum(scaled * gated, axis=0, keepdims=True)
    dgated = scaled * gain - gated * coef
    both = dgated * active
    acc[VOCAB + 5 : VOCAB + 6, :] += jnp.sum(both * silu_gate, axis=0, keepdims=True)
    dgate_out[...] = (both * scale * slope(gate, sig_gate)).astype(bf16)
    dconv = dgated * scale * silu_gate * slope(conv, sig_conv)
    dconv_out[...] = dconv

    @pl.when(step == 0)
    def _():
        first_out[...] = dconv[0:8, :]

    acc[VOCAB + 4 : VOCAB + 5, :] += jnp.sum(dconv, axis=0, keepdims=True)
    for k in range(KERNEL):
        tap = jnp.sum(dconv * xs[5 + k : 5 + k + tile, :], axis=0, keepdims=True)
        acc[VOCAB + k : VOCAB + k + 1, :] += tap


def back(gate_pre, x_pre, edge, params, m_loc, sums, resid_logits, targets, weight):
    tok, cols = x_pre.shape
    tile = tok // 4
    rows_spec = pl.BlockSpec((tile, cols), lambda i: (i, 0))

    def fixed(a):
        return pl.BlockSpec(a.shape, lambda i: (0, 0))

    def tokens(a):
        return pl.BlockSpec((a.shape[0], tile), lambda i: (0, i))

    return pl.pallas_call(
        functools.partial(back_kernel, weight, len(sums)),
        out_shape=[
            jax.ShapeDtypeStruct((tok, cols), bf16),
            jax.ShapeDtypeStruct((tok, cols), f32),
            jax.ShapeDtypeStruct((8, cols), f32),
            jax.ShapeDtypeStruct((VOCAB, tok), f32),
            jax.ShapeDtypeStruct((VOCAB + 8, cols), f32),
            jax.ShapeDtypeStruct((8, tok), f32),
        ],
        grid=(tok // tile,),
        in_specs=[rows_spec, rows_spec, fixed(edge), fixed(params), fixed(m_loc)]
        + [tokens(a) for a in (resid_logits, targets, *sums)],
        out_specs=[
            rows_spec,
            rows_spec,
            pl.BlockSpec((8, cols), lambda i: (0, 0)),
            pl.BlockSpec((VOCAB, tile), lambda i: (0, i)),
            pl.BlockSpec((VOCAB + 8, cols), lambda i: (0, 0)),
            pl.BlockSpec((8, tile), lambda i: (0, i)),
        ],
        scratch_shapes=[pltpu.VMEM((tile + 8, cols), f32)],
        compiler_params=pltpu.CompilerParams(vmem_limit_bytes=PROJ_VMEM),
        cost_estimate=LIGHT,
    )(gate_pre, x_pre, edge, params, m_loc, resid_logits, targets, *sums)


def blocks_kernel(sizes, idx, lhs, rhs, *outs):
    at = 0
    for out, size in zip(outs, sizes):
        for i in range(size):

            @pl.when(pl.program_id(0) == at)
            def _():
                total = jnp.dot(lhs[0], rhs[...], preferred_element_type=f32)
                out[i] = total.astype(bf16)

            at += 1


def block_grads(feat_t, rhs, places, begin, sizes, rows, vmem=16 * MIB):
    tok = feat_t.shape[2]
    cols = rhs.shape[1]

    def place(i, idx):
        return (idx[2 * (begin + i)], idx[2 * (begin + i) + 1], 0)

    return pl.pallas_call(
        functools.partial(blocks_kernel, sizes),
        out_shape=[jax.ShapeDtypeStruct((size, rows, cols), bf16) for size in sizes],
        grid_spec=pltpu.PrefetchScalarGridSpec(
            num_scalar_prefetch=1,
            grid=(sum(sizes),),
            in_specs=[
                pl.BlockSpec((1, rows, tok), place),
                pl.BlockSpec((tok, cols), lambda i, idx: (0, 0)),
            ],
            out_specs=[
                pl.BlockSpec((size, rows, cols), lambda i, idx: (0, 0, 0)) for size in sizes
            ],
        ),
        compiler_params=pltpu.CompilerParams(vmem_limit_bytes=vmem),
        cost_estimate=LIGHT,
    )(places, feat_t, rhs)


def dest_places(keys, rows, depth):
    slow, fast = seq_factors()
    me = lax.axis_index("seq")
    per_feat = depth // rows
    out = []
    for k, j in keys:
        dest = ((me // fast + k) % slow) * fast + (me % fast + j) % fast
        out += [(dest // per_feat) ^ lax.axis_index("chan"), dest % per_feat]
    return out


def slow_order():
    return [2, 3, 1, 0]


def per_device(
    targets, resid, w_gate_in, w_x_in, conv_weight, conv_bias, skip_d, norm_gain, w_out, w_head
):
    tok_rows = resid.shape[0]
    seq_count = lax.axis_size("seq")
    chan_count = lax.axis_size("chan")
    chan = lax.axis_index("chan")
    local_inner = w_gate_in.shape[1]
    w_rows = w_out.shape[0]
    halo = KERNEL - 1

    sources = gather_sources()
    slow, fast = seq_factors()
    order = slow_order()
    first, second = order[:2], order[2:]
    far = [(k, j) for pair in (first, second) for j in range(1, fast) for k in pair]
    near = [(k, 0) for k in order]
    per_feat = resid.shape[1] // w_rows
    idx = [chan ^ j for j in range(chan_count)]
    idx += [((i // per_feat) ^ chan) * per_feat + i % per_feat for i in sources]
    idx += dest_places(far + near, w_rows, resid.shape[1])
    n_idx = chan_count + seq_count
    n_use = fast // per_feat
    group_at = []
    for k in range(slow):
        group_at.append(len(idx))
        mine = sources[k * fast : (k + 1) * fast]
        idx += [(mine[0] // fast * n_use + m) ^ chan for m in range(n_use)]
        idx += [source % fast for source in mine]
    idx = jnp.concatenate([jnp.reshape(i, (1,)) for i in idx]).astype(jnp.int32)

    now = jnp.stack([w_gate_in, w_x_in])
    shards = []
    extra = [idx]
    for k in range(slow - 1):
        shards.append(now)
        came = [move_slow(now, 1)]
        came_fast = to_fast(now)
        if k == 0:
            feats = xor_gather(resid, "chan", 2)
            edge = shifted(resid[tok_rows - EDGE :], 1)
            head_t = w_head.T
            part_m = lax.dot_general(
                head_t, w_out, (((1,), (1,)), ((), ())), preferred_element_type=f32
            )
            part_r = lax.dot_general(
                head_t, resid, (((1,), (1,)), ((), ())), preferred_element_type=f32
            )
            early = jnp.concatenate([part_m, part_r], axis=1)
            early = early + flip(early, "chan", 1)
            head_scale = jnp.repeat(skip_d, HEADDIM)
            params = [conv_weight, conv_bias[None], head_scale[None]] + [norm_gain[None]] * 2
            params = jnp.concatenate(params, axis=0)
            extra = [idx, edge, early, params]
        if k == 1:
            bit = 2
            while bit < chan_count:
                early = early + flip(early, "chan", bit)
                bit *= 2
            own_m, resid_logits = early[:, :w_rows], early[:, w_rows:]
            pair_m = jnp.concatenate([own_m] + to_fast(own_m), axis=1)
            edges = xor_gather(after(edge, now), "chan", 2)
            extra = [pair_m, resid_logits] + feats + edges
        if k == 2:
            full = []
            for block in feats:
                full += [block, flip(block, "chan", 1)]
            feats, edges = full[:chan_count], full[chan_count:]
            part, part_edge = partial_products(
                [], feats, edges, shards[: 2 * fast], idx, group_at[:2], n_use
            )
            pair_m = after(pair_m, part)
            moved_m = [move_slow(pair_m, k) for k in range(1, slow)]
            extra = [pair_m, resid_logits, part, part_edge] + feats + edges
        came, came_fast, extra = sync(came, came_fast, extra)
        now = came[0]
        shards += came_fast
        if k == 0:
            idx, edge, early, params = extra
        if k == 1:
            pair_m, resid_logits, *feats = extra
    pair_m, resid_logits, part, part_edge = extra[:4]
    feats, edges = extra[4 : 4 + chan_count], extra[4 + chan_count : 4 + 2 * chan_count]
    shards.append(now)
    came_fast = to_fast(now)
    part, part_edge = partial_products(
        [part, part_edge], feats, edges, shards[2 * fast : 3 * fast], idx, group_at[2:3], n_use
    )
    feat_t = turned([after(feats[0], part)] + feats[1:])
    out_first = after(w_out, now)
    out_pair = jnp.stack([out_first, move_slow(out_first, 1)])
    out_third = move_slow(out_first, 3)
    per_chan = per_feat
    all_m = jnp.concatenate([pair_m] + moved_m, axis=1)
    pieces = [all_m[:, i * w_rows : (i + 1) * w_rows] for i in range(seq_count)]
    m_loc = jnp.concatenate(
        [picked(pieces, sources, chan * per_chan + i) for i in range(per_chan)], axis=1
    )
    came_fast, held = sync(came_fast, [now, out_pair, feat_t, part, m_loc])
    now, out_pair, feat_t, part, m_loc = held
    out_pair_fast = to_fast(out_pair)
    out_far = [move_slow(out_pair[1], 1), out_third]
    last = [now] + came_fast

    gate_pre, x_pre, normed, x_edge, sums = front(
        part, part_edge, params, m_loc, feats, edges, last, idx, group_at[3:], n_use
    )
    sums = [sums] + [flip(sums, "chan", j) for j in range(1, chan_count)]
    out_far = [after(out_far[0], sums[0])[None], after(out_far[1], *sums[1:])[None]]
    out_far_fast = to_fast(out_far[0]) + to_fast(out_far[1])
    loss_weight = 4.0 / math.sqrt(tok_rows * seq_count)
    normed_x = xor_gather(after(normed, *sums[1:]), "chan", 2)
    dgate, dconv, dfirst, dlogit, mid, squares = back(
        gate_pre, x_pre, x_edge, params, m_loc, sums, resid_logits, targets[None], loss_weight
    )
    future = shifted(dfirst, -1)[:halo]

    def far_grads(rhs, pair, vmem=16 * MIB):
        begin = n_idx // 2 + pair * (2 * fast - 2)
        return block_grads(feat_t, rhs, idx, begin, [2] * (fast - 1), w_rows, vmem)

    def near_grads(rhs):
        return block_grads(feat_t, rhs, idx, n_idx // 2 + len(far), [1] * slow, w_rows)

    def send_fast(blocks):
        return [move_fast(block, j) for j, block in enumerate(blocks, 1)]

    def total_of(own, came, i):
        return own[0].astype(f32) + sum(block[i].astype(f32) for block in came)

    hops = [1, 3]

    gate_first, held, out_pair_fast, out_far_fast = sync(
        far_grads(dgate, 0, PROJ_VMEM), [future, dconv, dlogit, dgate], out_pair_fast, out_far_fast
    )
    future, dconv, dlogit, dgate = held

    came = send_fast(gate_first)
    dpadded = jnp.concatenate([dconv, future], axis=0)
    dx_sum = jnp.zeros((tok_rows, local_inner), f32)
    for offset in range(KERNEL):
        dx_sum = (
            dx_sum + conv_weight[offset] * dpadded[halo - offset : halo - offset + tok_rows]
        )
    dx_pre = dx_sum.astype(bf16)
    gate_second = far_grads(dgate, 1)
    gate_own = near_grads(dgate)
    x_first = far_grads(dx_pre, 0)
    x_second = far_grads(dx_pre, 1)
    mid = after(mid, x_first[0], gate_own[0])
    mid_came = [move_slow(mid, k) for k in range(1, slow)]
    gate_first, gate_second, x_first, x_second, gate_own, normed_x, mid_came, held = sync(
        came, gate_second, x_first, x_second, gate_own, normed_x, mid_came, [dx_pre, mid]
    )
    dx_pre, mid = held
    mid = slow_total(mid, mid_came)

    came = send_fast(gate_second)
    gate_terms = [total_of(gate_own[i], gate_first, i).astype(bf16) for i in range(2)]
    gate_slow = [move_slow(term, by) for term, by in zip(gate_terms, hops)]
    normed_all = []
    for block in normed_x:
        normed_all += [block, flip(block, "chan", 1)]
    out_shards = [out_pair] + out_pair_fast
    counts = [[k * fast + j for k in (0, 1)] for j in range(fast)]
    for k in (2, 3):
        out_shards += [out_far[k - 2]] + out_far_fast[(k - 2) * (fast - 1) : (k - 1) * (fast - 1)]
        counts += [[k * fast + j] for j in range(fast)]
    raw = proj(normed_all, out_shards, counts, idx)
    gate_second, gate_slow[:1], x_first, x_second, held = sync(
        came, gate_slow[:1], x_first, x_second, [raw, dx_pre]
    )
    raw, dx_pre = held

    came = send_fast(x_first)
    term = total_of(gate_own[2], gate_second, 0) + gate_slow[0].astype(f32)
    gate_slow[0] = move_slow(term.astype(bf16), 1)
    inv = lax.rsqrt(squares[0] / INNER + 1e-05)[:, None]
    new_resid = (resid.astype(f32) + inv * raw.astype(f32)).astype(bf16)
    head_local = lax.dot_general(
        dlogit, new_resid.astype(f32), (((1,), (0,)), ((), ())), precision=HI
    )
    x_own = near_grads(dx_pre)
    mid_came = to_fast(mid)
    head_local = after(head_local, x_own[0])
    head_came = [move_slow(head_local, k) for k in range(1, slow)]
    x_first, x_second, x_own, gate_slow, mid_came, head_came, held = sync(
        came, x_second, x_own, gate_slow, mid_came, head_came, [mid, head_local]
    )
    mid, head_local = held
    mid = mid + sum(mid_came)
    head_local = slow_total(head_local, head_came)

    came = send_fast(x_second)
    x_terms = [total_of(x_own[i], x_first, i).astype(bf16) for i in range(2)]
    x_slow = [move_slow(term, by) for term, by in zip(x_terms, hops)]
    head_came = to_fast(after(head_local, *x_terms))
    g_pieces = xor_gather(after(mid[:VOCAB], *x_terms), "chan")
    x_second, x_slow, head_came, g_pieces = sync(came, x_slow, head_came, g_pieces)

    term = total_of(x_own[2], x_second, 0) + x_slow[0].astype(f32)
    x_slow[0] = move_slow(term.astype(bf16), 1)
    head_local = head_local + sum(head_came)
    grad_gate_in = total_of(gate_own[3], gate_second, 1) + sum(
        block.astype(f32) for block in gate_slow
    )
    rest = total_of(x_own[3], x_second, 1) + x_slow[1].astype(f32)
    grad_x_in = lax.optimization_barrier(rest) + x_slow[0].astype(f32)
    grad_head = head_local.T
    seq = lax.axis_index("seq")
    g_chan = picked(g_pieces, [chan ^ j for j in range(chan_count)], seq // per_chan)
    g_rows = lax.dynamic_slice_in_dim(g_chan, (seq % per_chan) * w_rows, w_rows, 1)
    grad_out = lax.dot_general(
        g_rows, w_head.T.astype(f32), (((0,), (0,)), ((), ())), precision=HI
    )
    tail = mid[VOCAB:]
    grad_skip = tail[KERNEL + 1].reshape(-1, HEADDIM).sum(axis=1)
    return (
        new_resid,
        grad_gate_in,
        grad_x_in,
        grad_out,
        grad_head,
        tail[:KERNEL],
        tail[KERNEL],
        grad_skip,
        tail[KERNEL + 2],
    )


def solution(mesh):
    return jax.shard_map(
        per_device,
        mesh=mesh,
        in_specs=(
            P("seq"),
            P("seq", "chan"),
            P("seq", "chan"),
            P("seq", "chan"),
            P(None, "chan"),
            P("chan"),
            P("chan"),
            P("chan"),
            P("seq", "chan"),
            P("chan", None),
        ),
        out_specs=(
            P("seq", "chan"),
            P("seq", "chan"),
            P("seq", "chan"),
            P("seq", "chan"),
            P("chan", None),
            P(None, "chan"),
            P("chan"),
            P("chan"),
            P("chan"),
        ),
        check_vma=False,
    )
```
